32 devices in a mesh: groups: 2 (over x), node: 16 (over z, y, core).
Axes of the slice: x: 2, y: 2, z: 4, core: 2. Of those that a mesh axis runs over, the one named last changes fastest.
Arguments:
- moe_input: bfloat16 [256, 3072], P(('groups', 'node')), parts along dimension 0, may hold values from -400 to 400
- norm_gain: bfloat16 [3072], replicated, may hold values from 0.099609375 to 1.8984375
- router_weight: bfloat16 [3072, 8], replicated, may hold values from -0.109375 to 0.109375
- routes: int32 [256, 2], P(('groups', 'node')), parts along dimension 0, may hold values from 0 to 7, all different within a row; in each aligned block of 8 rows (0 to 7, 8 to 15, ...) at most 4 rows name the same one
- gate_weight: bfloat16 [16, 3072, 4096], P('node'), may hold values from -0.109375 to 0.109375
- up_weight: bfloat16 [16, 3072, 4096], P('node'), may hold values from -0.109375 to 0.109375
- down_weight: bfloat16 [16, 4096, 3072], P('node'), may hold values from -0.0625 to 0.0625
- queries: bfloat16 [256, 3072], P(('groups', 'node')), parts along dimension 0, may hold values from -10 to 10
- key_cache: bfloat16 [256, 64, 512], P(('groups', 'node')), parts along dimension 0, may hold values from -10 to 10
- value_cache: bfloat16 [256, 64, 512], P(('groups', 'node')), parts along dimension 0, may hold values from -6 to 6
- new_keys: bfloat16 [256, 512], P(('groups', 'node')), parts along dimension 0, may hold values from -6 to 6
- new_values: bfloat16 [256, 512], P(('groups', 'node')), parts along dimension 0, may hold values from -6 to 6
- cache_lengths: int32 [256], P(('groups', 'node')), parts along dimension 0, may hold values from 1 to 64, as said below
Outputs:
- moe_output: bfloat16 [256, 3072], P(('groups', 'node')), parts along dimension 0
- attention_output: bfloat16 [256, 3072], P(('groups', 'node')), parts along dimension 0
The draws below stay inside these ranges and needn't reach their ends.
There are 2 independent parts, one for each index of `groups`. The reference program is written for one: setup_inputs(seed, part) draws one part's arguments, and reference() takes and returns one part's arrays. A program takes and returns all parts, laid end to end along the dimension named above; an argument that names none is the same for every part. Nothing has to cross between parts.
Inputs may be any that keep to these rules, and one draw needn't show every extreme that they name: `routes`: each row names 2 different experts. Among the 8 rows of one device no expert is named by more than 4 rows, a bound that some block reaches. `cache_lengths`: some row has 64.
All inputs are finite; a program needn't handle non-finite values.
Results may differ from the reference program's by a relative error of at most 0.0072.
Values may be sent and summed in bfloat16 or wider, within the bound.
No kernel may reach another device: no remote copies, remote signals or barrier semaphores. Data moves between devices by JAX's collectives and lax.ppermute only.
A program may use at most 192 MiB of HBM per device.

```python
import math
import jax
import jax.numpy as jnp
import numpy as np
from jax import lax

D = 3072
FF = 8192
E = 8
TOP = 2
HEADS = 24
KVH = 4
HD = 128
CACHE = 64
ROWS = 8
CAP = 4
SLICES = 2
GROUP = 6
ROWS_ALL = 128
N_NODE = 16


def draw_moe_input(key, part):
    key = jax.random.fold_in(key, 5)
    first, second, third = jax.random.split(key, 3)
    base = jnp.clip(jax.random.normal(first, (ROWS_ALL, D), jnp.float32), -4.0, 4.0)
    row_scale = jnp.exp(jax.random.uniform(second, (ROWS_ALL, 1), jnp.float32, 0.0, math.log(10.0)))
    column_scale = jnp.exp(jax.random.uniform(third, (1, D), jnp.float32, 0.0, math.log(10.0)))
    return (base * row_scale * column_scale).astype(jnp.bfloat16)


def draw_queries(key, part):
    key = jax.random.fold_in(key, 2)
    base = jnp.clip(jax.random.normal(key, (ROWS_ALL, HEADS * HD), jnp.float32), -6.0, 6.0)
    return base.astype(jnp.bfloat16)


def draw_key_cache(key, part):
    key = jax.random.fold_in(key, 3)
    base = jnp.clip(jax.random.normal(key, (ROWS_ALL, CACHE, KVH * HD), jnp.float32), -6.0, 6.0)
    return base.astype(jnp.bfloat16)


def draw_cache_lengths(key, part):
    key = jax.random.fold_in(key, 7)
    lengths = jax.random.randint(key, (ROWS_ALL,), 1, CACHE + 1, dtype=jnp.int32)
    return lengths.at[0].set(CACHE)


def level_of(key, extent, cuts, low, high):
    level, own = 1.0, jax.random.fold_in(key, 6)
    for dim, blocks in cuts:
        steps = jnp.exp(jax.random.uniform(jax.random.fold_in(own, dim), (blocks,), jnp.float32, low / len(cuts), high / len(cuts)))
        level = level * jnp.repeat(steps, extent[dim] // blocks).reshape([-1 if axis == dim else 1 for axis in range(len(extent))])
    return level


def assign_block(stream_key, own, number, rows, amount, top, bound, slope):
    ranking = jax.random.permutation(stream_key, amount)
    crowded, usual = portions_of(amount, rows * top, bound, slope, True), portions_of(amount, rows * top, bound, slope, False)
    places = jnp.arange(amount)

    def named(tallies, rotation):
        used = int((tallies > 0).sum())
        fixed = max(1, used // 4)
        passed = fixed + (places - fixed + rotation * (used - fixed)) % max(1, amount - fixed)
        return jnp.zeros((amount,), jnp.int32).at[ranking[jnp.where(places < fixed, places, passed)]].set(jnp.asarray(tallies, jnp.int32))

    tallies = jnp.where(number % 4 == 0, named(crowded, number // 4), named(usual, number - number // 4 - 1))
    mixed = jax.random.permutation(jax.random.fold_in(own, 3), amount)
    donor, taker = mixed[0:amount // 2 * 2:2], mixed[1:amount // 2 * 2:2]
    room = jnp.minimum(tallies[donor] - 1, bound - tallies[taker]) // 2
    room = jnp.where((donor == ranking[0]) | (taker == ranking[0]) | (tallies[taker] == 0), 0, jnp.maximum(room, 0))
    passed = jax.random.randint(jax.random.fold_in(own, 4), (amount // 2,), 0, 1 << 20) % (room + 1)
    tallies = tallies.at[donor].add(-passed).at[taker].add(passed)
    labels = jnp.searchsorted(jnp.cumsum(tallies), jnp.arange(rows * top), side="right").astype(jnp.int32)
    grid = labels.reshape(top, rows).T
    grid = grid[jax.random.permutation(jax.random.fold_in(own, 1), rows)]
    rotation = jax.random.randint(jax.random.fold_in(own, 2), (rows, 1), 0, top)
    return jnp.take_along_axis(grid, (jnp.arange(top)[None, :] + rotation) % top, axis=1)


def portions_of(amount, total, most, lean, full):
    loads = [(1 << 20) // math.isqrt(standing ** lean) + 1 for standing in range(1, amount + 1)]
    largest = most if full else min(most, max(-(-total // amount), total * loads[0] // sum(loads)))
    least = 1 if total - largest >= amount - 1 else 0
    holding, spare = [largest] + [least] * (amount - 1), total - largest - least * (amount - 1)
    while spare > 0:
        movable = [i for i in range(1, amount) if holding[i] < largest] or [i for i in range(1, amount) if holding[i] < most]
        whole, budget = sum([loads[i] for i in movable]), spare
        for i in movable:
            addition = min(most - holding[i], max(1, budget * loads[i] // whole), spare)
            holding[i] = holding[i] + addition
            spare = spare - addition
    return np.array(holding)


def noise(stream_key, extent, scale, limit, cuts=(), kind=jnp.bfloat16):
    entries = scale * jax.random.normal(stream_key, extent, jnp.float32)
    if cuts:
        entries = entries * level_of(stream_key, extent, cuts, -0.22, 0.18)
    return jnp.clip(entries, -limit, limit).astype(kind)


def setup_inputs(seed: int = 0, part: int = 0) -> dict:
    key_of = jax.random.split(jax.random.key(seed), 14)
    part_splits = jax.random.split(jax.random.fold_in(key_of[13], part), 14)
    moe_input = draw_moe_input(jax.random.fold_in(jax.random.fold_in(key_of[13], part), 71), part)
    norm_gain = jnp.clip(1.0 + 0.18 * jax.random.normal(key_of[1], (D,), jnp.float32), 0.099609375, 1.8984375).astype(jnp.bfloat16)
    router_weight = noise(key_of[2], (D, E), D ** -0.5, 0.109375)
    routes_keys = jax.random.split(jax.random.fold_in(part_splits[3], 1), ROWS_ALL // ROWS)
    routes_turns = jax.random.permutation(jax.random.fold_in(part_splits[3], 3), ROWS_ALL // ROWS)
    routes = jax.vmap(lambda own, number: assign_block(jax.random.fold_in(part_splits[3], 2), own, number, ROWS, E, TOP, CAP, 2))(routes_keys, routes_turns).reshape((ROWS_ALL, TOP))
    gate_weight = noise(key_of[4], (E * SLICES, D, FF // SLICES), D ** -0.5, 0.109375, ((0, 16),))
    up_weight = noise(key_of[5], (E * SLICES, D, FF // SLICES), D ** -0.5, 0.109375, ((0, 16),))
    down_weight = noise(key_of[6], (E * SLICES, FF // SLICES, D), FF ** -0.5, 0.0625, ((0, 16),))
    queries = draw_queries(jax.random.fold_in(jax.random.fold_in(key_of[13], part), 71), part)
    key_cache = draw_key_cache(jax.random.fold_in(jax.random.fold_in(key_of[13], part), 71), part)
    value_cache = noise(part_splits[9], (ROWS_ALL, CACHE, KVH * HD), 1.0, 6.0, ((0, 16),))
    new_keys = noise(part_splits[10], (ROWS_ALL, KVH * HD), 1.0, 6.0, ((0, 16),))
    new_values = noise(part_splits[11], (ROWS_ALL, KVH * HD), 1.0, 6.0, ((0, 16),))
    cache_lengths = draw_cache_lengths(jax.random.fold_in(jax.random.fold_in(key_of[13], part), 71), part)
    return dict(moe_input=moe_input, norm_gain=norm_gain, router_weight=router_weight, routes=routes, gate_weight=gate_weight, up_weight=up_weight, down_weight=down_weight, queries=queries, key_cache=key_cache, value_cache=value_cache, new_keys=new_keys, new_values=new_values, cache_lengths=cache_lengths)


def normalize(values, gain):
    wide = values.astype(jnp.float32)
    meansq = lax.optimization_barrier(jnp.mean(wide * wide, axis=-1, keepdims=True))
    return (wide * lax.rsqrt(meansq + 1e-05) * gain.astype(jnp.float32)).astype(jnp.bfloat16)

def route_terms(normed, router_weight, routes, experts):
    logits = jnp.dot(normed, router_weight, preferred_element_type=jnp.float32)
    onehot = (routes[:, :, None] == jnp.arange(experts, dtype=jnp.int32)[None, None, :]).astype(jnp.float32)
    picked = lax.optimization_barrier(jnp.sum(onehot * logits[:, None, :], axis=-1))
    weight = 1.0 / (1.0 + jnp.exp(picked[:, ::-1] - picked))
    member = lax.optimization_barrier(jnp.sum(onehot, axis=1))
    table = lax.optimization_barrier(jnp.sum(onehot * weight[:, :, None], axis=1))
    return (member, table)

def attention(queries, key_cache, value_cache, new_keys, new_values, cache_lengths):
    rows = queries.shape[0]
    scale = 1.0 / HD ** 0.5
    query = queries.astype(jnp.float32).reshape(rows, KVH, GROUP, HD)
    keys = key_cache.astype(jnp.float32).reshape(rows, CACHE, KVH, HD)
    vals = value_cache.astype(jnp.float32).reshape(rows, CACHE, KVH, HD)
    score = jnp.einsum('rkgh,rlkh->rkgl', query, keys) * scale
    live = jnp.arange(CACHE, dtype=jnp.int32)[None, :] < cache_lengths[:, None]
    score = jnp.where(live[:, None, None, :], score, -jnp.inf)
    own = jnp.einsum('rkgh,rkh->rkg', query, new_keys.astype(jnp.float32).reshape(rows, KVH, HD)) * scale
    top = jnp.maximum(lax.optimization_barrier(jnp.max(score, axis=-1)), own)
    weights = jnp.exp(score - top[..., None])
    own_weight = jnp.exp(own - top)
    total = lax.optimization_barrier(jnp.sum(weights, axis=-1)) + own_weight
    probs = (weights / total[..., None]).astype(jnp.bfloat16).astype(jnp.float32)
    own_prob = (own_weight / total).astype(jnp.bfloat16).astype(jnp.float32)
    mixed = jnp.einsum('rkgl,rlkh->rkgh', probs, vals)
    mixed = mixed + own_prob[..., None] * new_values.astype(jnp.float32).reshape(rows, KVH, 1, HD)
    return mixed.reshape(rows, HEADS * HD).astype(jnp.bfloat16)

def reference(moe_input, norm_gain, router_weight, routes, gate_weight, up_weight, down_weight, queries, key_cache, value_cache, new_keys, new_values, cache_lengths):
    normed = normalize(moe_input, norm_gain)
    member, table = route_terms(normed, router_weight, routes, E)
    member = member.reshape(N_NODE, ROWS, E)
    table = table.reshape(N_NODE, ROWS, E)
    ranks = jnp.cumsum(member, axis=1) - member
    blocks = normed.reshape(N_NODE, ROWS, D).astype(jnp.float32)
    slots = jnp.arange(CAP, dtype=jnp.float32)

    def one_expert(carry, expert):
        hit = lax.dynamic_index_in_dim(member, expert, 2, keepdims=False)
        rank = lax.dynamic_index_in_dim(ranks, expert, 2, keepdims=False)
        weight = lax.dynamic_index_in_dim(table, expert, 2, keepdims=False)
        select = hit[:, None, :] * (rank[:, None, :] == slots[None, :, None]).astype(jnp.float32)
        buffer = jnp.einsum('scr,srd->scd', select, blocks).astype(jnp.bfloat16).reshape(N_NODE * CAP, D)

        def one_slice(total, piece):
            index = expert * SLICES + piece
            gate = jnp.dot(buffer, gate_weight[index], preferred_element_type=jnp.float32)
            upper = jnp.dot(buffer, up_weight[index], preferred_element_type=jnp.float32)
            hidden = (jax.nn.silu(gate) * upper).astype(jnp.bfloat16)
            part = jnp.dot(hidden, down_weight[index], preferred_element_type=jnp.float32).astype(jnp.bfloat16)
            return (total + part.astype(jnp.float32), None)
        summed, unused = lax.scan(one_slice, jnp.zeros((N_NODE * CAP, D), jnp.float32), jnp.arange(SLICES, dtype=jnp.int32))
        weighted = select * weight[:, None, :]
        share = jnp.einsum('scr,scd->srd', weighted, summed.reshape(N_NODE, CAP, D), precision=lax.Precision.HIGHEST)
        return (carry + share, None)
    mixed, unused = lax.scan(one_expert, jnp.zeros((N_NODE, ROWS, D), jnp.float32), jnp.arange(E, dtype=jnp.int32))
    moe_output = mixed.reshape(N_NODE * ROWS, D).astype(jnp.bfloat16)
    attention_output = attention(queries, key_cache, value_cache, new_keys, new_values, cache_lengths)
    return (moe_output, attention_output)
```

```python
import functools

import jax
import jax.numpy as jnp
from jax import lax
from jax.experimental import pallas as pl
from jax.experimental.pallas import tpu as pltpu
from jax.sharding import PartitionSpec as P

HEADS = 24
KVH = 4
HD = 128
GROUP = 6
TILE = 256
MIB = 1 << 20
F32 = jnp.float32
BF16 = jnp.bfloat16
WHOLE = pl.BlockSpec(memory_space=pltpu.VMEM)
ANY = pl.BlockSpec(memory_space=pl.ANY)


def normalize(values, gain):
    wide = values.astype(jnp.float32)
    meansq = jnp.mean(wide * wide, axis=-1, keepdims=True)
    return (wide * lax.rsqrt(meansq + 1e-05) * gain.astype(jnp.float32)).astype(jnp.bfloat16)


def send_back(partial_rows, experts, slices):
    returned = lax.all_to_all(partial_rows, "node", split_axis=0, concat_axis=0, tiled=True)
    count = returned.shape[1]
    width = returned.shape[2]
    return jnp.sum(returned.reshape(experts, slices, count, width).astype(jnp.float32), axis=1)


def run_expert(received, gate_slice, up_slice, down_slice):
    senders, count, width = received.shape
    flat = received.reshape(senders * count, width)
    gate = jnp.dot(flat, gate_slice, preferred_element_type=jnp.float32)
    upper = jnp.dot(flat, up_slice, preferred_element_type=jnp.float32)
    hidden = (jax.nn.silu(gate) * upper).astype(jnp.bfloat16)
    part = jnp.dot(hidden, down_slice, preferred_element_type=jnp.float32).astype(jnp.bfloat16)
    return part.reshape(senders, count, width)


def plain_attention(queries, key_cache, value_cache, new_keys, new_values, cache_lengths):
    rows = queries.shape[0]
    length = key_cache.shape[1]
    scale = 1.0 / HD**0.5
    query = queries.reshape(rows, KVH, GROUP, HD)
    keys = key_cache.reshape(rows, length, KVH, HD)
    vals = value_cache.reshape(rows, length, KVH, HD)
    score = jnp.einsum("rkgh,rlkh->rkgl", query, keys, preferred_element_type=jnp.float32) * scale
    live = jnp.arange(length, dtype=jnp.int32)[None, :] < cache_lengths[:, None]
    score = jnp.where(live[:, None, None, :], score, -jnp.inf)
    own = (
        jnp.einsum(
            "rkgh,rkh->rkg",
            query,
            new_keys.reshape(rows, KVH, HD),
            preferred_element_type=jnp.float32,
        )
        * scale
    )
    top = jnp.maximum(jnp.max(score, axis=-1), own)
    weights = jnp.exp(score - top[..., None])
    own_weight = jnp.exp(own - top)
    total = jnp.sum(weights, axis=-1) + own_weight
    probs = (weights / total[..., None]).astype(jnp.bfloat16)
    own_prob = (own_weight / total).astype(jnp.bfloat16)
    mixed = jnp.einsum("rkgl,rlkh->rkgh", probs, vals, preferred_element_type=jnp.float32)
    mixed = mixed + own_prob.astype(jnp.float32)[..., None] * new_values.reshape(
        rows, KVH, 1, HD
    ).astype(jnp.float32)
    return mixed.reshape(rows, HEADS * HD).astype(jnp.bfloat16)


def plain_shards(
    moe_input,
    norm_gain,
    router_weight,
    routes,
    gate_weight,
    up_weight,
    down_weight,
    queries,
    key_cache,
    value_cache,
    new_keys,
    new_values,
    cache_lengths,
):
    rows, width = moe_input.shape
    experts = router_weight.shape[1]
    devices = lax.axis_size("node")
    slices = devices // experts
    capacity = rows // 2
    normed = normalize(moe_input, norm_gain)
    logits = jnp.dot(normed, router_weight, preferred_element_type=jnp.float32)
    onehot_int = (routes[:, :, None] == jnp.arange(experts, dtype=jnp.int32)[None, None, :]).astype(
        jnp.int32
    )
    onehot = onehot_int.astype(jnp.float32)
    picked = jnp.sum(onehot * logits[:, None, :], axis=-1)
    weight = 1.0 / (1.0 + jnp.exp(picked[:, ::-1] - picked))
    member_int = jnp.sum(onehot_int, axis=1)
    ranks_int = jnp.cumsum(member_int, axis=0) - member_int
    slots = jnp.arange(capacity, dtype=jnp.int32)
    select = (
        jnp.transpose(member_int)[:, None, :]
        * (jnp.transpose(ranks_int)[:, None, :] == slots[None, :, None]).astype(jnp.int32)
    ).astype(jnp.bfloat16)
    gate_slice = gate_weight[0]
    up_slice = up_weight[0]
    down_slice = down_weight[0]
    packed = jnp.einsum("ecr,rd->ecd", select, normed, preferred_element_type=jnp.float32).astype(
        jnp.bfloat16
    )
    outgoing = jnp.broadcast_to(packed[:, None], (experts, slices, capacity, width)).reshape(
        devices, capacity, width
    )
    summed = send_back(
        run_expert(
            lax.all_to_all(outgoing, "node", split_axis=0, concat_axis=0, tiled=True),
            gate_slice,
            up_slice,
            down_slice,
        ),
        experts,
        slices,
    )
    slot_of = jnp.sum(onehot_int * ranks_int[:, None, :], axis=-1)
    position = routes * capacity + slot_of
    picked_rows = summed.reshape(experts * capacity, width)[position]
    moe_output = jnp.sum(weight[:, :, None] * picked_rows, axis=1).astype(jnp.bfloat16)
    attention_output = plain_attention(
        queries, key_cache, value_cache, new_keys, new_values, cache_lengths
    )
    return (moe_output, attention_output)


def select_slots(routes, experts, capacity):
    lines, rows = experts.shape
    named = [routes[k : k + 1, :] == experts for k in range(2)]
    member = jnp.where(named[0] | named[1], 1.0, 0.0)
    before = lax.broadcasted_iota(jnp.int32, (rows, rows), 0) < lax.broadcasted_iota(
        jnp.int32, (rows, rows), 1
    )
    rank = jnp.dot(member, jnp.where(before, 1.0, 0.0), preferred_element_type=F32)
    slot = (lax.broadcasted_iota(jnp.int32, (lines, rows), 0) % capacity).astype(F32)
    return [flag & (rank == slot) for flag in named]


def line_experts(column, capacity, lines, rows):
    line = lax.broadcasted_iota(jnp.int32, (lines, rows), 0)
    block = 2 * capacity
    return ((line // block) ^ column) * 2 + (line % block) // capacity


def pack_kernel(capacity, x_hbm, routes_hbm, *refs):
    *out_refs, x_ref, routes_ref, sems = refs
    copies = [
        pltpu.make_async_copy(routes_hbm, routes_ref, sems.at[0]),
        pltpu.make_async_copy(x_hbm, x_ref, sems.at[1]),
    ]
    for copy in copies:
        copy.start()
    for copy in copies:
        copy.wait()
    column = lax.axis_index("node") // 4
    rows = x_ref.shape[0]
    block = out_refs[0].shape[0]
    lines = block * len(out_refs)
    first, second = select_slots(
        routes_ref[...], line_experts(column, capacity, lines, rows), capacity
    )
    chosen = jnp.where(first | second, 1.0, 0.0).astype(BF16)
    packed = jnp.dot(chosen, x_ref[...], preferred_element_type=F32)
    for k, out_ref in enumerate(out_refs):
        out_ref[...] = packed[k * block : (k + 1) * block].astype(BF16)


def halves_kernel(capacity, *refs):
    *in_refs, _, keep_ref, send_ref = refs
    mine = (lax.axis_index("node") // 2) % 2
    block = 2 * capacity
    lines = len(in_refs) * block
    half = lines // 2
    out_line = lax.broadcasted_iota(jnp.int32, (lines, lines), 0)
    in_line = lax.broadcasted_iota(jnp.int32, (lines, lines), 1)
    which = jnp.where(out_line < half, mine, 1 - mine)
    within = out_line % half
    source = (within // capacity) * block + which * capacity + within % capacity
    move = jnp.where(in_line == source, 1.0, 0.0).astype(BF16)
    values = jnp.concatenate([ref[...] for ref in in_refs], axis=0)
    moved = jnp.dot(move, values, preferred_element_type=F32)
    keep_ref[...] = moved[:half].astype(BF16)
    send_ref[...] = moved[half:].astype(BF16)


def blocks_kernel(capacity, mine_ref, other_ref, *out_refs):
    mine = (lax.axis_index("node") // 2) % 2
    block = 2 * capacity
    lines = block * len(out_refs)
    half = lines // 2
    out_line = lax.broadcasted_iota(jnp.int32, (lines, lines), 0)
    in_line = lax.broadcasted_iota(jnp.int32, (lines, lines), 1)
    which = jnp.where((out_line % block) // capacity == mine, 0, 1)
    source = which * half + (out_line // block) * capacity + out_line % capacity
    move = jnp.where(in_line == source, 1.0, 0.0).astype(BF16)
    values = jnp.concatenate([mine_ref[...], other_ref[...]], axis=0)
    moved = jnp.dot(move, values, preferred_element_type=F32)
    for k, out_ref in enumerate(out_refs):
        out_ref[...] = moved[k * block : (k + 1) * block].astype(BF16)


def add_kernel(left0_ref, left1_ref, right0_ref, right1_ref, out0_ref, out1_ref):
    out0_ref[...] = (left0_ref[...] + right0_ref[...].astype(F32)).astype(BF16)
    out1_ref[...] = (left1_ref[...] + right1_ref[...].astype(F32)).astype(BF16)


def rms(values, gain):
    wide = values.astype(F32)
    meansq = jnp.mean(wide * wide, axis=-1, keepdims=True)
    return (wide * lax.rsqrt(meansq + 1e-05) * gain.astype(F32).reshape(1, -1)).astype(BF16)


def attention(lengths_ref, q_ref, k_ref, v_ref, nk_ref, nv_ref, out_ref):
    rows = q_ref.shape[0]
    length = k_ref.shape[1]
    groups = k_ref.shape[2] // HD
    per_group = q_ref.shape[1] // HD // groups
    lines, columns = per_group * rows, rows * length
    scale = 1.0 / HD**0.5
    row = lax.broadcasted_iota(jnp.int32, (lines, 1), 0) % rows
    count = jnp.zeros((lines, 1), jnp.int32)
    for r in range(rows):
        count = jnp.where(row == r, lengths_ref[r], count)
    position = lax.broadcasted_iota(jnp.int32, (lines, columns), 1) - row * length
    live = (position >= 0) & (position < count)
    for g in range(groups):
        lanes = slice(g * HD, (g + 1) * HD)
        heads = [slice(h * HD, (h + 1) * HD) for h in range(g * per_group, (g + 1) * per_group)]
        query = jnp.concatenate([q_ref[:, head].astype(F32) for head in heads], axis=0)
        keys = k_ref[:, :, lanes].reshape(columns, HD)
        values = v_ref[:, :, lanes].reshape(columns, HD)
        new_key = jnp.concatenate([nk_ref[:, lanes].astype(F32)] * per_group, axis=0)
        new_value = jnp.concatenate([nv_ref[:, lanes].astype(F32)] * per_group, axis=0)
        score = (
            lax.dot_general(
                query.astype(BF16), keys, (((1,), (1,)), ((), ())), preferred_element_type=F32
            )
            * scale
        )
        own = jnp.sum(query * new_key, axis=-1, keepdims=True) * scale
        score = jnp.where(live, score, -jnp.inf)
        top = jnp.maximum(jnp.max(score, axis=-1, keepdims=True), own)
        weights = jnp.exp(score - top)
        own_weight = jnp.exp(own - top)
        total = jnp.sum(weights, axis=-1, keepdims=True) + own_weight
        probs = (weights / total).astype(BF16)
        own_prob = (own_weight / total).astype(BF16).astype(F32)
        mixed = jnp.dot(probs, values, preferred_element_type=F32) + own_prob * new_value
        for j, head in enumerate(heads):
            out_ref[:, head] = mixed[j * rows : (j + 1) * rows].astype(BF16)


def side_kernel(
    lengths_ref,
    q_ref,
    k_hbm,
    v_hbm,
    nk_ref,
    nv_ref,
    x_ref,
    gain_ref,
    router_ref,
    out_ref,
    logits_ref,
    k_ref,
    v_ref,
    sems,
):
    copies = [
        pltpu.make_async_copy(k_hbm, k_ref, sems.at[0]),
        pltpu.make_async_copy(v_hbm, v_ref, sems.at[1]),
    ]
    for copy in copies:
        copy.start()
    logits_ref[...] = lax.dot_general(
        router_ref[...],
        rms(x_ref[...], gain_ref[...]),
        (((1,), (1,)), ((), ())),
        preferred_element_type=F32,
    )
    for copy in copies:
        copy.wait()
    attention(lengths_ref, q_ref, k_ref, v_ref, nk_ref, nv_ref, out_ref)


def down_copy(down_ref, buf, sems, tile, slot):
    return pltpu.make_async_copy(
        down_ref.at[0, pl.ds(pl.multiple_of(tile * TILE, TILE), TILE), :],
        buf.at[slot],
        sems.at[slot],
    )


def expert_kernel(
    slots,
    a_ref,
    b_ref,
    c_ref,
    d_ref,
    gain_ref,
    gate_ref,
    up_ref,
    down_ref,
    own0_ref,
    own1_ref,
    far0_ref,
    far1_ref,
    x_buf,
    total,
    down_buf,
    sems,
):
    tiles = gate_ref.shape[2] // TILE
    part = a_ref.shape[0]
    for tile in range(min(slots, tiles)):
        down_copy(down_ref, down_buf, sems, tile, tile).start()
    for i, ref in enumerate((a_ref, b_ref, c_ref, d_ref)):
        x_buf[i * part : (i + 1) * part, :] = rms(ref[...], gain_ref[...])
    total[...] = jnp.zeros_like(total)

    def step(tile, carry):
        slot = lax.rem(tile, slots)
        cols = pl.ds(pl.multiple_of(tile * TILE, TILE), TILE)
        x = x_buf[...]
        gated = jnp.dot(x, gate_ref[0, :, cols], preferred_element_type=F32)
        upper = jnp.dot(x, up_ref[0, :, cols], preferred_element_type=F32)
        hidden = (gated / (1.0 + jnp.exp(-gated)) * upper).astype(BF16)
        down_copy(down_ref, down_buf, sems, tile, slot).wait()
        total[...] += jnp.dot(hidden, down_buf[slot], preferred_element_type=F32)

        @pl.when(tile + slots < tiles)
        def _():
            down_copy(down_ref, down_buf, sems, tile + slots, slot).start()

        return carry

    lax.fori_loop(0, tiles, step, 0)
    own0_ref[...] = total[:part]
    own1_ref[...] = total[part : 2 * part]
    far0_ref[...] = total[2 * part : 3 * part].astype(BF16)
    far1_ref[...] = total[3 * part :].astype(BF16)


def combine_kernel(capacity, routes_ref, logits_ref, *refs):
    *in_refs, out_ref = refs
    column = lax.axis_index("node") // 4
    routes = routes_ref[...]
    logits = logits_ref[...]
    expert = lax.broadcasted_iota(jnp.int32, logits.shape, 0)
    picked = [
        jnp.sum(jnp.where(routes[k : k + 1, :] == expert, logits, 0.0), axis=0, keepdims=True)
        for k in range(2)
    ]
    block, rows = in_refs[0].shape[0], routes.shape[1]
    lines = block * len(in_refs)
    hits = select_slots(routes, line_experts(column, capacity, lines, rows), capacity)
    table = jnp.zeros(hits[0].shape, F32)
    for k in range(2):
        weight = 1.0 / (1.0 + jnp.exp(picked[1 - k] - picked[k]))
        table += jnp.where(hits[k], weight, 0.0)
    high = table.astype(BF16)
    rest = table - high.astype(F32)
    middle = rest.astype(BF16)
    low = (rest - middle.astype(F32)).astype(BF16)
    values = jnp.concatenate([ref[...] for ref in in_refs], axis=0)
    terms = [
        lax.dot_general(term, values, (((0,), (0,)), ((), ())), preferred_element_type=F32)
        for term in (low, middle, high)
    ]
    out_ref[...] = (terms[0] + terms[1] + terms[2]).astype(BF16)


def call(kernel, name, outs, ins, operands, scratch=(), limit=4, cost=None):
    return pl.pallas_call(
        kernel,
        out_shape=outs,
        in_specs=ins,
        out_specs=tuple(WHOLE for _ in outs) if isinstance(outs, tuple) else WHOLE,
        scratch_shapes=list(scratch),
        compiler_params=pltpu.CompilerParams(vmem_limit_bytes=limit * MIB),
        cost_estimate=cost,
        name=name,
    )(*operands)


def exchange(values, bits):
    size = lax.axis_size("node")
    return lax.ppermute(values, "node", [(i, i ^ bits) for i in range(size)])


def paired_shards(
    moe_input,
    norm_gain,
    router_weight,
    routes,
    gate_weight,
    up_weight,
    down_weight,
    queries,
    key_cache,
    value_cache,
    new_keys,
    new_values,
    cache_lengths,
):
    rows, width = moe_input.shape
    experts = router_weight.shape[1]
    capacity = rows // 2
    columns = lax.axis_size("node") // 4
    block = 2 * capacity
    half = columns * capacity
    named = routes.T
    gain = norm_gain

    def like(lines, dtype=BF16):
        return jax.ShapeDtypeStruct((lines, width), dtype)

    def held(lines, dtype=BF16):
        return pltpu.VMEM((lines, width), dtype)

    packed = call(
        functools.partial(pack_kernel, capacity),
        "pack",
        (like(block),) * columns,
        [pl.BlockSpec(memory_space=pltpu.HBM)] * 2,
        [pltpu.with_memory_space_constraint(array, pltpu.HBM) for array in (moe_input, named)],
        [
            pltpu.VMEM(moe_input.shape, BF16),
            pltpu.VMEM(named.shape, jnp.int32),
            pltpu.SemaphoreType.DMA((2,)),
        ],
        cost=pl.CostEstimate(flops=10**11, bytes_accessed=64 * MIB, transcendentals=0),
    )
    blocks = [packed[0]] + [exchange(packed[k], 4 * k) for k in range(1, columns)]
    attended, logits = call(
        side_kernel,
        "side",
        (like(rows), jax.ShapeDtypeStruct((experts, rows), F32)),
        [pl.BlockSpec(memory_space=pltpu.SMEM), WHOLE, ANY, ANY] + [WHOLE] * 5,
        (
            cache_lengths,
            queries,
            key_cache,
            value_cache,
            new_keys,
            new_values,
            moe_input,
            gain,
            router_weight.T,
        ),
        [
            pltpu.VMEM(key_cache.shape, BF16),
            pltpu.VMEM(value_cache.shape, BF16),
            pltpu.SemaphoreType.DMA((2,)),
        ],
        cost=pl.CostEstimate(flops=10**8, bytes_accessed=4 * MIB, transcendentals=0),
    )
    keep, send = call(
        functools.partial(halves_kernel, capacity),
        "halves",
        (like(half),) * 2,
        [WHOLE] * columns + [ANY],
        (*blocks, logits),
    )
    far_keep = exchange(keep, 1)
    across = exchange(send, 2)
    far_across = exchange(across, 1)
    slots = 3
    own0, own1, far0, far1 = call(
        functools.partial(expert_kernel, slots),
        "expert",
        (held(half, F32), held(half, F32), held(half), held(half)),
        [WHOLE] * 7 + [ANY],
        (
            keep,
            across,
            far_keep,
            far_across,
            gain,
            pltpu.with_memory_space_constraint(gate_weight, pltpu.VMEM),
            pltpu.with_memory_space_constraint(up_weight, pltpu.VMEM),
            down_weight,
        ),
        [
            pltpu.VMEM((4 * half, width), BF16),
            pltpu.VMEM((4 * half, width), F32),
            pltpu.VMEM((slots, TILE, width), BF16),
            pltpu.SemaphoreType.DMA((slots,)),
        ],
        limit=9,
    )
    back0, back1 = exchange(far0, 1), exchange(far1, 1)
    sum0, sum1 = call(
        add_kernel,
        "add",
        (like(half),) * 2,
        [WHOLE] * 4,
        (
            pltpu.with_memory_space_constraint(own0, pltpu.VMEM),
            pltpu.with_memory_space_constraint(own1, pltpu.VMEM),
            back0,
            back1,
        ),
    )
    other = exchange(sum1, 2)
    results = call(
        functools.partial(blocks_kernel, capacity),
        "blocks",
        (like(block),) * columns,
        [WHOLE] * 2,
        (sum0, other),
    )
    results = [results[0]] + [exchange(results[k], 4 * k) for k in range(1, columns)]
    moe_output = call(
        functools.partial(combine_kernel, capacity),
        "combine",
        like(rows),
        [WHOLE] * (2 + columns),
        (named, logits, *results),
    )
    return moe_output, attended


def shards(*arrays):
    experts = arrays[2].shape[1]
    devices = lax.axis_size("node")
    units = arrays[4].shape[2]
    if devices == 2 * experts and devices % 8 == 0 and units % TILE == 0 and arrays[0].shape[0] == 8:
        return paired_shards(*arrays)
    return plain_shards(*arrays)


def solution(mesh):
    in_specs = (
        P(("groups", "node"), None),
        P(),
        P(),
        P(("groups", "node"), None),
        P("node", None, None),
        P("node", None, None),
        P("node", None, None),
        P(("groups", "node"), None),
        P(("groups", "node"), None, None),
        P(("groups", "node"), None, None),
        P(("groups", "node"), None),
        P(("groups", "node"), None),
        P(("groups", "node")),
    )
    out_specs = (P(("groups", "node"), None), P(("groups", "node"), None))
    return jax.shard_map(shards, mesh=mesh, in_specs=in_specs, out_specs=out_specs, check_vma=False)
```

```python
import functools

import jax
import jax.numpy as jnp
from jax import lax
from jax.experimental import pallas as pl
from jax.experimental.pallas import tpu as pltpu
from jax.sharding import PartitionSpec as P

HEADS = 24
KVH = 4
HD = 128
GROUP = 6
TILE = 512
MIB = 1 << 20
F32 = jnp.float32
BF16 = jnp.bfloat16
WHOLE = pl.BlockSpec(memory_space=pltpu.VMEM)
ANY = pl.BlockSpec(memory_space=pl.ANY)


def normalize(values, gain):
    wide = values.astype(jnp.float32)
    meansq = jnp.mean(wide * wide, axis=-1, keepdims=True)
    return (wide * lax.rsqrt(meansq + 1e-05) * gain.astype(jnp.float32)).astype(jnp.bfloat16)


def send_back(partial_rows, experts, slices):
    returned = lax.all_to_all(partial_rows, "node", split_axis=0, concat_axis=0, tiled=True)
    count = returned.shape[1]
    width = returned.shape[2]
    return jnp.sum(returned.reshape(experts, slices, count, width).astype(jnp.float32), axis=1)


def run_expert(received, gate_slice, up_slice, down_slice):
    senders, count, width = received.shape
    flat = received.reshape(senders * count, width)
    gate = jnp.dot(flat, gate_slice, preferred_element_type=jnp.float32)
    upper = jnp.dot(flat, up_slice, preferred_element_type=jnp.float32)
    hidden = (jax.nn.silu(gate) * upper).astype(jnp.bfloat16)
    part = jnp.dot(hidden, down_slice, preferred_element_type=jnp.float32).astype(jnp.bfloat16)
    return part.reshape(senders, count, width)


def plain_attention(queries, key_cache, value_cache, new_keys, new_values, cache_lengths):
    rows = queries.shape[0]
    length = key_cache.shape[1]
    scale = 1.0 / HD**0.5
    query = queries.reshape(rows, KVH, GROUP, HD)
    keys = key_cache.reshape(rows, length, KVH, HD)
    vals = value_cache.reshape(rows, length, KVH, HD)
    score = jnp.einsum("rkgh,rlkh->rkgl", query, keys, preferred_element_type=jnp.float32) * scale
    live = jnp.arange(length, dtype=jnp.int32)[None, :] < cache_lengths[:, None]
    score = jnp.where(live[:, None, None, :], score, -jnp.inf)
    own = (
        jnp.einsum(
            "rkgh,rkh->rkg",
            query,
            new_keys.reshape(rows, KVH, HD),
            preferred_element_type=jnp.float32,
        )
        * scale
    )
    top = jnp.maximum(jnp.max(score, axis=-1), own)
    weights = jnp.exp(score - top[..., None])
    own_weight = jnp.exp(own - top)
    total = jnp.sum(weights, axis=-1) + own_weight
    probs = (weights / total[..., None]).astype(jnp.bfloat16)
    own_prob = (own_weight / total).astype(jnp.bfloat16)
    mixed = jnp.einsum("rkgl,rlkh->rkgh", probs, vals, preferred_element_type=jnp.float32)
    mixed = mixed + own_prob.astype(jnp.float32)[..., None] * new_values.reshape(
        rows, KVH, 1, HD
    ).astype(jnp.float32)
    return mixed.reshape(rows, HEADS * HD).astype(jnp.bfloat16)


def plain_shards(
    moe_input,
    norm_gain,
    router_weight,
    routes,
    gate_weight,
    up_weight,
    down_weight,
    queries,
    key_cache,
    value_cache,
    new_keys,
    new_values,
    cache_lengths,
):
    rows, width = moe_input.shape
    experts = router_weight.shape[1]
    devices = lax.axis_size("node")
    slices = devices // experts
    capacity = rows // 2
    normed = normalize(moe_input, norm_gain)
    logits = jnp.dot(normed, router_weight, preferred_element_type=jnp.float32)
    onehot_int = (routes[:, :, None] == jnp.arange(experts, dtype=jnp.int32)[None, None, :]).astype(
        jnp.int32
    )
    onehot = onehot_int.astype(jnp.float32)
    picked = jnp.sum(onehot * logits[:, None, :], axis=-1)
    weight = 1.0 / (1.0 + jnp.exp(picked[:, ::-1] - picked))
    member_int = jnp.sum(onehot_int, axis=1)
    ranks_int = jnp.cumsum(member_int, axis=0) - member_int
    slots = jnp.arange(capacity, dtype=jnp.int32)
    select = (
        jnp.transpose(member_int)[:, None, :]
        * (jnp.transpose(ranks_int)[:, None, :] == slots[None, :, None]).astype(jnp.int32)
    ).astype(jnp.bfloat16)
    gate_slice = gate_weight[0]
    up_slice = up_weight[0]
    down_slice = down_weight[0]
    packed = jnp.einsum("ecr,rd->ecd", select, normed, preferred_element_type=jnp.float32).astype(
        jnp.bfloat16
    )
    outgoing = jnp.broadcast_to(packed[:, None], (experts, slices, capacity, width)).reshape(
        devices, capacity, width
    )
    summed = send_back(
        run_expert(
            lax.all_to_all(outgoing, "node", split_axis=0, concat_axis=0, tiled=True),
            gate_slice,
            up_slice,
            down_slice,
        ),
        experts,
        slices,
    )
    slot_of = jnp.sum(onehot_int * ranks_int[:, None, :], axis=-1)
    position = routes * capacity + slot_of
    picked_rows = summed.reshape(experts * capacity, width)[position]
    moe_output = jnp.sum(weight[:, :, None] * picked_rows, axis=1).astype(jnp.bfloat16)
    attention_output = plain_attention(
        queries, key_cache, value_cache, new_keys, new_values, cache_lengths
    )
    return (moe_output, attention_output)


def select_slots(routes, experts, capacity):
    lines, rows = experts.shape
    named = [routes[k : k + 1, :] == experts for k in range(2)]
    member = jnp.where(named[0] | named[1], 1.0, 0.0)
    before = lax.broadcasted_iota(jnp.int32, (rows, rows), 0) < lax.broadcasted_iota(
        jnp.int32, (rows, rows), 1
    )
    rank = jnp.dot(member, jnp.where(before, 1.0, 0.0), preferred_element_type=F32)
    slot = (lax.broadcasted_iota(jnp.int32, (lines, rows), 0) % capacity).astype(F32)
    return [flag & (rank == slot) for flag in named]


def line_experts(column, capacity, lines, rows):
    line = lax.broadcasted_iota(jnp.int32, (lines, rows), 0)
    block = 2 * capacity
    return ((line // block) ^ column) * 2 + (line % block) // capacity


def pack_kernel(capacity, x_hbm, routes_hbm, *refs):
    *out_refs, x_ref, routes_ref, sems = refs
    copies = [
        pltpu.make_async_copy(routes_hbm, routes_ref, sems.at[0]),
        pltpu.make_async_copy(x_hbm, x_ref, sems.at[1]),
    ]
    for copy in copies:
        copy.start()
    for copy in copies:
        copy.wait()
    column = lax.axis_index("node") // 4
    rows = x_ref.shape[0]
    block = out_refs[0].shape[0]
    lines = block * len(out_refs)
    first, second = select_slots(
        routes_ref[...], line_experts(column, capacity, lines, rows), capacity
    )
    chosen = jnp.where(first | second, 1.0, 0.0).astype(BF16)
    packed = jnp.dot(chosen, x_ref[...], preferred_element_type=F32)
    for k, out_ref in enumerate(out_refs):
        out_ref[...] = packed[k * block : (k + 1) * block].astype(BF16)


def halves_kernel(capacity, *refs):
    *in_refs, _, keep_ref, send_ref = refs
    mine = (lax.axis_index("node") // 2) % 2
    block = 2 * capacity
    lines = len(in_refs) * block
    half = lines // 2
    out_line = lax.broadcasted_iota(jnp.int32, (lines, lines), 0)
    in_line = lax.broadcasted_iota(jnp.int32, (lines, lines), 1)
    which = jnp.where(out_line < half, mine, 1 - mine)
    within = out_line % half
    source = (within // capacity) * block + which * capacity + within % capacity
    move = jnp.where(in_line == source, 1.0, 0.0).astype(BF16)
    values = jnp.concatenate([ref[...] for ref in in_refs], axis=0)
    moved = jnp.dot(move, values, preferred_element_type=F32)
    keep_ref[...] = moved[:half].astype(BF16)
    send_ref[...] = moved[half:].astype(BF16)


def blocks_kernel(capacity, mine_ref, other_ref, *out_refs):
    mine = (lax.axis_index("node") // 2) % 2
    block = 2 * capacity
    lines = block * len(out_refs)
    half = lines // 2
    out_line = lax.broadcasted_iota(jnp.int32, (lines, lines), 0)
    in_line = lax.broadcasted_iota(jnp.int32, (lines, lines), 1)
    which = jnp.where((out_line % block) // capacity == mine, 0, 1)
    source = which * half + (out_line // block) * capacity + out_line % capacity
    move = jnp.where(in_line == source, 1.0, 0.0).astype(BF16)
    values = jnp.concatenate([mine_ref[...], other_ref[...]], axis=0)
    moved = jnp.dot(move, values, preferred_element_type=F32)
    for k, out_ref in enumerate(out_refs):
        out_ref[...] = moved[k * block : (k + 1) * block].astype(BF16)


def add_kernel(left0_ref, left1_ref, right0_ref, right1_ref, out0_ref, out1_ref):
    out0_ref[...] = (left0_ref[...] + right0_ref[...].astype(F32)).astype(BF16)
    out1_ref[...] = (left1_ref[...] + right1_ref[...].astype(F32)).astype(BF16)


def rms(values, gain):
    wide = values.astype(F32)
    meansq = jnp.mean(wide * wide, axis=-1, keepdims=True)
    return (wide * lax.rsqrt(meansq + 1e-05) * gain.astype(F32).reshape(1, -1)).astype(BF16)


def attention(lengths_ref, q_ref, k_ref, v_ref, nk_ref, nv_ref, out_ref):
    rows = q_ref.shape[0]
    length = k_ref.shape[1]
    groups = k_ref.shape[2] // HD
    per_group = q_ref.shape[1] // HD // groups
    lines, columns = per_group * rows, rows * length
    scale = 1.0 / HD**0.5
    row = lax.broadcasted_iota(jnp.int32, (lines, 1), 0) % rows
    count = jnp.zeros((lines, 1), jnp.int32)
    for r in range(rows):
        count = jnp.where(row == r, lengths_ref[r], count)
    position = lax.broadcasted_iota(jnp.int32, (lines, columns), 1) - row * length
    live = (position >= 0) & (position < count)
    for g in range(groups):
        lanes = slice(g * HD, (g + 1) * HD)
        heads = [slice(h * HD, (h + 1) * HD) for h in range(g * per_group, (g + 1) * per_group)]
        query = jnp.concatenate([q_ref[:, head].astype(F32) for head in heads], axis=0)
        keys = k_ref[:, :, lanes].reshape(columns, HD)
        values = v_ref[:, :, lanes].reshape(columns, HD)
        new_key = jnp.concatenate([nk_ref[:, lanes].astype(F32)] * per_group, axis=0)
        new_value = jnp.concatenate([nv_ref[:, lanes].astype(F32)] * per_group, axis=0)
        score = (
            lax.dot_general(
                query.astype(BF16), keys, (((1,), (1,)), ((), ())), preferred_element_type=F32
            )
            * scale
        )
        own = jnp.sum(query * new_key, axis=-1, keepdims=True) * scale
        score = jnp.where(live, score, -jnp.inf)
        top = jnp.maximum(jnp.max(score, axis=-1, keepdims=True), own)
        weights = jnp.exp(score - top)
        own_weight = jnp.exp(own - top)
        total = jnp.sum(weights, axis=-1, keepdims=True) + own_weight
        probs = (weights / total).astype(BF16)
        own_prob = (own_weight / total).astype(BF16).astype(F32)
        mixed = jnp.dot(probs, values, preferred_element_type=F32) + own_prob * new_value
        for j, head in enumerate(heads):
            out_ref[:, head] = mixed[j * rows : (j + 1) * rows].astype(BF16)


def side_kernel(
    lengths_ref,
    q_ref,
    k_hbm,
    v_hbm,
    nk_ref,
    nv_ref,
    x_ref,
    gain_ref,
    router_ref,
    out_ref,
    logits_ref,
    k_ref,
    v_ref,
    sems,
):
    copies = [
        pltpu.make_async_copy(k_hbm, k_ref, sems.at[0]),
        pltpu.make_async_copy(v_hbm, v_ref, sems.at[1]),
    ]
    for copy in copies:
        copy.start()
    logits_ref[...] = lax.dot_general(
        router_ref[...],
        rms(x_ref[...], gain_ref[...]),
        (((1,), (1,)), ((), ())),
        preferred_element_type=F32,
    )
    for copy in copies:
        copy.wait()
    attention(lengths_ref, q_ref, k_ref, v_ref, nk_ref, nv_ref, out_ref)


def down_copy(down_ref, buf, sems, tile, slot):
    return pltpu.make_async_copy(
        down_ref.at[0, pl.ds(pl.multiple_of(tile * TILE, TILE), TILE), :],
        buf.at[slot],
        sems.at[slot],
    )


def expert_kernel(
    slots,
    a_ref,
    b_ref,
    c_ref,
    d_ref,
    gain_ref,
    gate_ref,
    up_ref,
    down_ref,
    own0_ref,
    own1_ref,
    far0_ref,
    far1_ref,
    x_buf,
    hidden,
    total,
    down_buf,
    sems,
):
    tiles = gate_ref.shape[2] // TILE
    part = a_ref.shape[0]
    lines = total.shape[0]
    for tile in range(min(slots, tiles)):
        down_copy(down_ref, down_buf, sems, tile, tile).start()
    for i, ref in enumerate((a_ref, b_ref, c_ref, d_ref)):
        x_buf[i * part : (i + 1) * part, :] = rms(ref[...], gain_ref[...])
    x_buf[lines:, :] = jnp.zeros_like(x_buf[lines:, :])
    total[...] = jnp.zeros_like(total)

    def activate(tile):
        cols = pl.ds(pl.multiple_of(tile * TILE, TILE), TILE)
        x = x_buf[...]
        gated = jnp.dot(x, gate_ref[0, :, cols], preferred_element_type=F32)
        upper = jnp.dot(x, up_ref[0, :, cols], preferred_element_type=F32)
        return (gated / (1.0 + jnp.exp(-gated)) * upper).astype(BF16)

    def project(tile):
        slot = lax.rem(tile, slots)
        down_copy(down_ref, down_buf, sems, tile, slot).wait()
        return jnp.dot(hidden[lax.rem(tile, 2)], down_buf[slot], preferred_element_type=F32)

    def refill(tile):
        @pl.when(tile + slots < tiles)
        def _():
            down_copy(down_ref, down_buf, sems, tile + slots, lax.rem(tile, slots)).start()

    hidden[0] = activate(0)

    def step(tile, carry):
        product = project(tile - 1)
        hidden[lax.rem(tile, 2)] = activate(tile)
        total[...] += product[:lines]
        refill(tile - 1)
        return carry

    lax.fori_loop(1, tiles, step, 0)
    result = total[...] + project(tiles - 1)[:lines]
    own0_ref[...] = result[:part]
    own1_ref[...] = result[part : 2 * part]
    far0_ref[...] = result[2 * part : 3 * part].astype(BF16)
    far1_ref[...] = result[3 * part :].astype(BF16)


def combine_kernel(capacity, routes_ref, logits_ref, *refs):
    *in_refs, out_ref = refs
    column = lax.axis_index("node") // 4
    routes = routes_ref[...]
    logits = logits_ref[...]
    expert = lax.broadcasted_iota(jnp.int32, logits.shape, 0)
    picked = [
        jnp.sum(jnp.where(routes[k : k + 1, :] == expert, logits, 0.0), axis=0, keepdims=True)
        for k in range(2)
    ]
    block, rows = in_refs[0].shape[0], routes.shape[1]
    lines = block * len(in_refs)
    hits = select_slots(routes, line_experts(column, capacity, lines, rows), capacity)
    table = jnp.zeros(hits[0].shape, F32)
    for k in range(2):
        weight = 1.0 / (1.0 + jnp.exp(picked[1 - k] - picked[k]))
        table += jnp.where(hits[k], weight, 0.0)
    high = table.astype(BF16)
    rest = table - high.astype(F32)
    middle = rest.astype(BF16)
    low = (rest - middle.astype(F32)).astype(BF16)
    values = jnp.concatenate([ref[...] for ref in in_refs], axis=0)
    terms = [
        lax.dot_general(term, values, (((0,), (0,)), ((), ())), preferred_element_type=F32)
        for term in (low, middle, high)
    ]
    out_ref[...] = (terms[0] + terms[1] + terms[2]).astype(BF16)


def call(kernel, name, outs, ins, operands, scratch=(), limit=4, cost=None):
    return pl.pallas_call(
        kernel,
        out_shape=outs,
        in_specs=ins,
        out_specs=tuple(WHOLE for _ in outs) if isinstance(outs, tuple) else WHOLE,
        scratch_shapes=list(scratch),
        compiler_params=pltpu.CompilerParams(vmem_limit_bytes=limit * MIB),
        cost_estimate=cost,
        name=name,
    )(*operands)


def exchange(values, bits):
    size = lax.axis_size("node")
    return lax.ppermute(values, "node", [(i, i ^ bits) for i in range(size)])


def paired_shards(
    moe_input,
    norm_gain,
    router_weight,
    routes,
    gate_weight,
    up_weight,
    down_weight,
    queries,
    key_cache,
    value_cache,
    new_keys,
    new_values,
    cache_lengths,
):
    rows, width = moe_input.shape
    experts = router_weight.shape[1]
    capacity = rows // 2
    columns = lax.axis_size("node") // 4
    block = 2 * capacity
    half = columns * capacity
    named = routes.T
    gain = norm_gain

    def like(lines, dtype=BF16):
        return jax.ShapeDtypeStruct((lines, width), dtype)

    def held(lines, dtype=BF16):
        return pltpu.VMEM((lines, width), dtype)

    packed = call(
        functools.partial(pack_kernel, capacity),
        "pack",
        (like(block),) * columns,
        [pl.BlockSpec(memory_space=pltpu.HBM)] * 2,
        [pltpu.with_memory_space_constraint(array, pltpu.HBM) for array in (moe_input, named)],
        [
            pltpu.VMEM(moe_input.shape, BF16),
            pltpu.VMEM(named.shape, jnp.int32),
            pltpu.SemaphoreType.DMA((2,)),
        ],
        cost=pl.CostEstimate(flops=10**11, bytes_accessed=64 * MIB, transcendentals=0),
    )
    blocks = [packed[0]] + [exchange(packed[k], 4 * k) for k in range(1, columns)]
    attended, logits = call(
        side_kernel,
        "side",
        (like(rows), jax.ShapeDtypeStruct((experts, rows), F32)),
        [pl.BlockSpec(memory_space=pltpu.SMEM), WHOLE, ANY, ANY] + [WHOLE] * 5,
        (
            cache_lengths,
            queries,
            key_cache,
            value_cache,
            new_keys,
            new_values,
            moe_input,
            gain,
            router_weight.T,
        ),
        [
            pltpu.VMEM(key_cache.shape, BF16),
            pltpu.VMEM(value_cache.shape, BF16),
            pltpu.SemaphoreType.DMA((2,)),
        ],
        cost=pl.CostEstimate(flops=10**8, bytes_accessed=4 * MIB, transcendentals=0),
    )
    keep, send = call(
        functools.partial(halves_kernel, capacity),
        "halves",
        (like(half),) * 2,
        [WHOLE] * columns + [ANY],
        (*blocks, logits),
    )
    far_keep = exchange(keep, 1)
    across = exchange(send, 2)
    far_across = exchange(across, 1)
    slots = 2
    lines = max(4 * half, 128)
    own0, own1, far0, far1 = call(
        functools.partial(expert_kernel, slots),
        "expert",
        (held(half, F32), held(half, F32), held(half), held(half)),
        [WHOLE] * 7 + [ANY],
        (
            *[
                pltpu.with_memory_space_constraint(part, pltpu.VMEM)
                for part in (keep, across, far_keep, far_across)
            ],
            gain,
            pltpu.with_memory_space_constraint(gate_weight, pltpu.VMEM),
            pltpu.with_memory_space_constraint(up_weight, pltpu.VMEM),
            down_weight,
        ),
        [
            pltpu.VMEM((lines, width), BF16),
            pltpu.VMEM((2, lines, TILE), BF16),
            pltpu.VMEM((4 * half, width), F32),
            pltpu.VMEM((slots, TILE, width), BF16),
            pltpu.SemaphoreType.DMA((slots,)),
        ],
        limit=12,
    )
    back0, back1 = exchange(far0, 1), exchange(far1, 1)
    sum0, sum1 = call(
        add_kernel,
        "add",
        (like(half),) * 2,
        [WHOLE] * 4,
        (
            pltpu.with_memory_space_constraint(own0, pltpu.VMEM),
            pltpu.with_memory_space_constraint(own1, pltpu.VMEM),
            back0,
            back1,
        ),
    )
    other = exchange(sum1, 2)
    results = call(
        functools.partial(blocks_kernel, capacity),
        "blocks",
        (like(block),) * columns,
        [WHOLE] * 2,
        (sum0, other),
    )
    results = [results[0]] + [exchange(results[k], 4 * k) for k in range(1, columns)]
    moe_output = call(
        functools.partial(combine_kernel, capacity),
        "combine",
        like(rows),
        [WHOLE] * (2 + columns),
        (named, logits, *results),
    )
    return moe_output, attended


def shards(*arrays):
    experts = arrays[2].shape[1]
    devices = lax.axis_size("node")
    units = arrays[4].shape[2]
    if devices == 2 * experts and devices % 8 == 0 and units % TILE == 0 and arrays[0].shape[0] == 8:
        return paired_shards(*arrays)
    return plain_shards(*arrays)


def solution(mesh):
    in_specs = (
        P(("groups", "node"), None),
        P(),
        P(),
        P(("groups", "node"), None),
        P("node", None, None),
        P("node", None, None),
        P("node", None, None),
        P(("groups", "node"), None),
        P(("groups", "node"), None, None),
        P(("groups", "node"), None, None),
        P(("groups", "node"), None),
        P(("groups", "node"), None),
        P(("groups", "node")),
    )
    out_specs = (P(("groups", "node"), None), P(("groups", "node"), None))
    return jax.shard_map(shards, mesh=mesh, in_specs=in_specs, out_specs=out_specs, check_vma=False)
```

```python
import functools

import jax
import jax.numpy as jnp
from jax import lax
from jax.experimental import pallas as pl
from jax.experimental.pallas import tpu as pltpu
from jax.sharding import PartitionSpec as P

HEADS = 24
KVH = 4
HD = 128
GROUP = 6
TILE = 512
MIB = 1 << 20
F32 = jnp.float32
BF16 = jnp.bfloat16
WHOLE = pl.BlockSpec(memory_space=pltpu.VMEM)
ANY = pl.BlockSpec(memory_space=pl.ANY)


def normalize(values, gain):
    wide = values.astype(jnp.float32)
    meansq = jnp.mean(wide * wide, axis=-1, keepdims=True)
    return (wide * lax.rsqrt(meansq + 1e-05) * gain.astype(jnp.float32)).astype(jnp.bfloat16)


def send_back(partial_rows, experts, slices):
    returned = lax.all_to_all(partial_rows, "node", split_axis=0, concat_axis=0, tiled=True)
    count = returned.shape[1]
    width = returned.shape[2]
    return jnp.sum(returned.reshape(experts, slices, count, width).astype(jnp.float32), axis=1)


def run_expert(received, gate_slice, up_slice, down_slice):
    senders, count, width = received.shape
    flat = received.reshape(senders * count, width)
    gate = jnp.dot(flat, gate_slice, preferred_element_type=jnp.float32)
    upper = jnp.dot(flat, up_slice, preferred_element_type=jnp.float32)
    hidden = (jax.nn.silu(gate) * upper).astype(jnp.bfloat16)
    part = jnp.dot(hidden, down_slice, preferred_element_type=jnp.float32).astype(jnp.bfloat16)
    return part.reshape(senders, count, width)


def plain_attention(queries, key_cache, value_cache, new_keys, new_values, cache_lengths):
    rows = queries.shape[0]
    length = key_cache.shape[1]
    scale = 1.0 / HD**0.5
    query = queries.reshape(rows, KVH, GROUP, HD)
    keys = key_cache.reshape(rows, length, KVH, HD)
    vals = value_cache.reshape(rows, length, KVH, HD)
    score = jnp.einsum("rkgh,rlkh->rkgl", query, keys, preferred_element_type=jnp.float32) * scale
    live = jnp.arange(length, dtype=jnp.int32)[None, :] < cache_lengths[:, None]
    score = jnp.where(live[:, None, None, :], score, -jnp.inf)
    own = (
        jnp.einsum(
            "rkgh,rkh->rkg",
            query,
            new_keys.reshape(rows, KVH, HD),
            preferred_element_type=jnp.float32,
        )
        * scale
    )
    top = jnp.maximum(jnp.max(score, axis=-1), own)
    weights = jnp.exp(score - top[..., None])
    own_weight = jnp.exp(own - top)
    total = jnp.sum(weights, axis=-1) + own_weight
    probs = (weights / total[..., None]).astype(jnp.bfloat16)
    own_prob = (own_weight / total).astype(jnp.bfloat16)
    mixed = jnp.einsum("rkgl,rlkh->rkgh", probs, vals, preferred_element_type=jnp.float32)
    mixed = mixed + own_prob.astype(jnp.float32)[..., None] * new_values.reshape(
        rows, KVH, 1, HD
    ).astype(jnp.float32)
    return mixed.reshape(rows, HEADS * HD).astype(jnp.bfloat16)


def plain_shards(
    moe_input,
    norm_gain,
    router_weight,
    routes,
    gate_weight,
    up_weight,
    down_weight,
    queries,
    key_cache,
    value_cache,
    new_keys,
    new_values,
    cache_lengths,
):
    rows, width = moe_input.shape
    experts = router_weight.shape[1]
    devices = lax.axis_size("node")
    slices = devices // experts
    capacity = rows // 2
    normed = normalize(moe_input, norm_gain)
    logits = jnp.dot(normed, router_weight, preferred_element_type=jnp.float32)
    onehot_int = (routes[:, :, None] == jnp.arange(experts, dtype=jnp.int32)[None, None, :]).astype(
        jnp.int32
    )
    onehot = onehot_int.astype(jnp.float32)
    picked = jnp.sum(onehot * logits[:, None, :], axis=-1)
    weight = 1.0 / (1.0 + jnp.exp(picked[:, ::-1] - picked))
    member_int = jnp.sum(onehot_int, axis=1)
    ranks_int = jnp.cumsum(member_int, axis=0) - member_int
    slots = jnp.arange(capacity, dtype=jnp.int32)
    select = (
        jnp.transpose(member_int)[:, None, :]
        * (jnp.transpose(ranks_int)[:, None, :] == slots[None, :, None]).astype(jnp.int32)
    ).astype(jnp.bfloat16)
    gate_slice = gate_weight[0]
    up_slice = up_weight[0]
    down_slice = down_weight[0]
    packed = jnp.einsum("ecr,rd->ecd", select, normed, preferred_element_type=jnp.float32).astype(
        jnp.bfloat16
    )
    outgoing = jnp.broadcast_to(packed[:, None], (experts, slices, capacity, width)).reshape(
        devices, capacity, width
    )
    summed = send_back(
        run_expert(
            lax.all_to_all(outgoing, "node", split_axis=0, concat_axis=0, tiled=True),
            gate_slice,
            up_slice,
            down_slice,
        ),
        experts,
        slices,
    )
    slot_of = jnp.sum(onehot_int * ranks_int[:, None, :], axis=-1)
    position = routes * capacity + slot_of
    picked_rows = summed.reshape(experts * capacity, width)[position]
    moe_output = jnp.sum(weight[:, :, None] * picked_rows, axis=1).astype(jnp.bfloat16)
    attention_output = plain_attention(
        queries, key_cache, value_cache, new_keys, new_values, cache_lengths
    )
    return (moe_output, attention_output)


def select_slots(routes, experts, capacity):
    lines, rows = experts.shape
    named = [routes[k : k + 1, :] == experts for k in range(2)]
    member = jnp.where(named[0] | named[1], 1.0, 0.0)
    before = lax.broadcasted_iota(jnp.int32, (rows, rows), 0) < lax.broadcasted_iota(
        jnp.int32, (rows, rows), 1
    )
    rank = jnp.dot(member, jnp.where(before, 1.0, 0.0), preferred_element_type=F32)
    slot = (lax.broadcasted_iota(jnp.int32, (lines, rows), 0) % capacity).astype(F32)
    return [flag & (rank == slot) for flag in named]


def line_experts(column, capacity, lines, rows):
    line = lax.broadcasted_iota(jnp.int32, (lines, rows), 0)
    block = 2 * capacity
    return ((line // block) ^ column) * 2 + (line % block) // capacity


def pack_kernel(capacity, x_hbm, routes_hbm, *refs):
    *out_refs, x_ref, routes_ref, sems = refs
    copies = [
        pltpu.make_async_copy(routes_hbm, routes_ref, sems.at[0]),
        pltpu.make_async_copy(x_hbm, x_ref, sems.at[1]),
    ]
    for copy in copies:
        copy.start()
    for copy in copies:
        copy.wait()
    column = lax.axis_index("node") // 4
    rows = x_ref.shape[0]
    block = out_refs[0].shape[0]
    lines = block * len(out_refs)
    first, second = select_slots(
        routes_ref[...], line_experts(column, capacity, lines, rows), capacity
    )
    chosen = jnp.where(first | second, 1.0, 0.0).astype(BF16)
    packed = jnp.dot(chosen, x_ref[...], preferred_element_type=F32)
    for k, out_ref in enumerate(out_refs):
        out_ref[...] = packed[k * block : (k + 1) * block].astype(BF16)


def halves_kernel(capacity, *refs):
    *in_refs, _, keep_ref, send_ref = refs
    mine = (lax.axis_index("node") // 2) % 2
    block = 2 * capacity
    lines = len(in_refs) * block
    half = lines // 2
    out_line = lax.broadcasted_iota(jnp.int32, (lines, lines), 0)
    in_line = lax.broadcasted_iota(jnp.int32, (lines, lines), 1)
    which = jnp.where(out_line < half, mine, 1 - mine)
    within = out_line % half
    source = (within // capacity) * block + which * capacity + within % capacity
    move = jnp.where(in_line == source, 1.0, 0.0).astype(BF16)
    values = jnp.concatenate([ref[...] for ref in in_refs], axis=0)
    moved = jnp.dot(move, values, preferred_element_type=F32)
    keep_ref[...] = moved[:half].astype(BF16)
    send_ref[...] = moved[half:].astype(BF16)


def merge_kernel(capacity, own_ref, far_ref, *out_refs):
    block = 2 * capacity
    lines = block * len(out_refs)
    out_line = lax.broadcasted_iota(jnp.int32, (lines, lines), 0)
    in_line = lax.broadcasted_iota(jnp.int32, (lines, lines), 1)
    which = (out_line % block) // capacity
    source = which * (lines // 2) + (out_line // block) * capacity + out_line % capacity
    move = jnp.where(in_line == source, 1.0, 0.0).astype(BF16)
    values = (own_ref[...] + far_ref[...].astype(F32)).astype(BF16)
    moved = jnp.dot(move, values, preferred_element_type=F32)
    for k, out_ref in enumerate(out_refs):
        out_ref[...] = moved[k * block : (k + 1) * block].astype(BF16)


def rms(values, gain):
    wide = values.astype(F32)
    meansq = jnp.mean(wide * wide, axis=-1, keepdims=True)
    return (wide * lax.rsqrt(meansq + 1e-05) * gain.astype(F32).reshape(1, -1)).astype(BF16)


def attention(lengths_ref, q_ref, k_ref, v_ref, nk_ref, nv_ref, out_ref):
    rows = q_ref.shape[0]
    length = k_ref.shape[1]
    groups = k_ref.shape[2] // HD
    per_group = q_ref.shape[1] // HD // groups
    lines, columns = per_group * rows, rows * length
    scale = 1.0 / HD**0.5
    row = lax.broadcasted_iota(jnp.int32, (lines, 1), 0) % rows
    count = jnp.zeros((lines, 1), jnp.int32)
    for r in range(rows):
        count = jnp.where(row == r, lengths_ref[r], count)
    position = lax.broadcasted_iota(jnp.int32, (lines, columns), 1) - row * length
    live = (position >= 0) & (position < count)
    for g in range(groups):
        lanes = slice(g * HD, (g + 1) * HD)
        heads = [slice(h * HD, (h + 1) * HD) for h in range(g * per_group, (g + 1) * per_group)]
        query = jnp.concatenate([q_ref[:, head].astype(F32) for head in heads], axis=0)
        keys = k_ref[:, :, lanes].reshape(columns, HD)
        values = v_ref[:, :, lanes].reshape(columns, HD)
        new_key = jnp.concatenate([nk_ref[:, lanes].astype(F32)] * per_group, axis=0)
        new_value = jnp.concatenate([nv_ref[:, lanes].astype(F32)] * per_group, axis=0)
        score = (
            lax.dot_general(
                query.astype(BF16), keys, (((1,), (1,)), ((), ())), preferred_element_type=F32
            )
            * scale
        )
        own = jnp.sum(query * new_key, axis=-1, keepdims=True) * scale
        score = jnp.where(live, score, -jnp.inf)
        top = jnp.maximum(jnp.max(score, axis=-1, keepdims=True), own)
        weights = jnp.exp(score - top)
        own_weight = jnp.exp(own - top)
        total = jnp.sum(weights, axis=-1, keepdims=True) + own_weight
        probs = (weights / total).astype(BF16)
        own_prob = (own_weight / total).astype(BF16).astype(F32)
        mixed = jnp.dot(probs, values, preferred_element_type=F32) + own_prob * new_value
        for j, head in enumerate(heads):
            out_ref[:, head] = mixed[j * rows : (j + 1) * rows].astype(BF16)


def side_kernel(
    capacity,
    lengths_ref,
    q_ref,
    k_hbm,
    v_hbm,
    nk_ref,
    nv_ref,
    x_ref,
    gain_ref,
    router_ref,
    routes_ref,
    out_ref,
    table_ref,
    k_ref,
    v_ref,
    sems,
):
    copies = [
        pltpu.make_async_copy(k_hbm, k_ref, sems.at[0]),
        pltpu.make_async_copy(v_hbm, v_ref, sems.at[1]),
    ]
    for copy in copies:
        copy.start()
    logits = lax.dot_general(
        router_ref[...],
        rms(x_ref[...], gain_ref[...]),
        (((1,), (1,)), ((), ())),
        preferred_element_type=F32,
    )
    table_ref[...] = slot_weights(capacity, routes_ref[...], logits, table_ref.shape[0])
    for copy in copies:
        copy.wait()
    attention(lengths_ref, q_ref, k_ref, v_ref, nk_ref, nv_ref, out_ref)


def down_copy(down_ref, buf, sems, tile, slot):
    return pltpu.make_async_copy(
        down_ref.at[0, pl.ds(pl.multiple_of(tile * TILE, TILE), TILE), :],
        buf.at[slot],
        sems.at[slot],
    )


def expert_kernel(
    slots,
    a_ref,
    b_ref,
    c_ref,
    d_ref,
    gain_ref,
    gate_ref,
    up_ref,
    down_ref,
    own_ref,
    far_ref,
    x_buf,
    hidden,
    total,
    down_buf,
    sems,
):
    tiles = gate_ref.shape[2] // TILE
    part = a_ref.shape[0]
    lines = total.shape[0]
    for tile in range(min(slots, tiles)):
        down_copy(down_ref, down_buf, sems, tile, tile).start()
    for i, ref in enumerate((a_ref, b_ref, c_ref, d_ref)):
        x_buf[i * part : (i + 1) * part, :] = rms(ref[...], gain_ref[...])
    x_buf[lines:, :] = jnp.zeros_like(x_buf[lines:, :])
    total[...] = jnp.zeros_like(total)

    def activate(tile):
        cols = pl.ds(pl.multiple_of(tile * TILE, TILE), TILE)
        x = x_buf[...]
        gated = jnp.dot(x, gate_ref[0, :, cols], preferred_element_type=F32)
        upper = jnp.dot(x, up_ref[0, :, cols], preferred_element_type=F32)
        return (gated / (1.0 + jnp.exp(-gated)) * upper).astype(BF16)

    def project(tile):
        slot = lax.rem(tile, slots)
        down_copy(down_ref, down_buf, sems, tile, slot).wait()
        return jnp.dot(hidden[lax.rem(tile, 2)], down_buf[slot], preferred_element_type=F32)

    def refill(tile):
        @pl.when(tile + slots < tiles)
        def _():
            down_copy(down_ref, down_buf, sems, tile + slots, lax.rem(tile, slots)).start()

    hidden[0] = activate(0)

    def step(tile, carry):
        product = project(tile - 1)
        hidden[lax.rem(tile, 2)] = activate(tile)
        total[...] += product[:lines]
        refill(tile - 1)
        return carry

    lax.fori_loop(1, tiles, step, 0)
    result = total[...] + project(tiles - 1)[:lines]
    own_ref[...] = result[: 2 * part]
    far_ref[...] = result[2 * part :].astype(BF16)


def slot_weights(capacity, routes, logits, lines):
    column, mine = lax.axis_index("node") // 4, (lax.axis_index("node") // 2) % 2
    shape = (lines, routes.shape[1])
    line = lax.broadcasted_iota(jnp.int32, shape, 0)
    block = 2 * capacity
    which = (line % block) // capacity
    experts = ((line // block) ^ column) * 2 + jnp.where(which == 0, mine, 1 - mine)
    expert = lax.broadcasted_iota(jnp.int32, logits.shape, 0)
    picked = [
        jnp.sum(jnp.where(routes[k : k + 1, :] == expert, logits, 0.0), axis=0, keepdims=True)
        for k in range(2)
    ]
    hits = select_slots(routes, experts, capacity)
    table = jnp.zeros(shape, F32)
    for k in range(2):
        weight = 1.0 / (1.0 + jnp.exp(picked[1 - k] - picked[k]))
        table += jnp.where(hits[k], weight, 0.0)
    return table


def mix_kernel(capacity, table_ref, other_ref, *refs):
    *in_refs, own_ref, send_ref = refs
    which = lax.broadcasted_iota(jnp.int32, table_ref.shape, 0) % (2 * capacity) // capacity
    table = jnp.concatenate(
        [
            jnp.where(which == 0, table_ref[...], 0.0),
            jnp.where(which == 1, other_ref[...], 0.0),
        ],
        axis=1,
    )
    high = table.astype(BF16)
    rest = table - high.astype(F32)
    middle = rest.astype(BF16)
    low = (rest - middle.astype(F32)).astype(BF16)
    values = jnp.concatenate([ref[...] for ref in in_refs], axis=0)
    terms = [
        lax.dot_general(term, values, (((0,), (0,)), ((), ())), preferred_element_type=F32)
        for term in (low, middle, high)
    ]
    mixed = terms[0] + terms[1] + terms[2]
    rows = own_ref.shape[0]
    own_ref[...] = mixed[:rows]
    send_ref[...] = mixed[rows:].astype(BF16)


def final_kernel(own_ref, other_ref, out_ref):
    out_ref[...] = (own_ref[...] + other_ref[...].astype(F32)).astype(BF16)


def call(kernel, name, outs, ins, operands, scratch=(), limit=4, cost=None):
    return pl.pallas_call(
        kernel,
        out_shape=outs,
        in_specs=ins,
        out_specs=tuple(WHOLE for _ in outs) if isinstance(outs, tuple) else WHOLE,
        scratch_shapes=list(scratch),
        compiler_params=pltpu.CompilerParams(vmem_limit_bytes=limit * MIB),
        cost_estimate=cost,
        name=name,
    )(*operands)


def exchange(values, bits):
    size = lax.axis_size("node")
    return lax.ppermute(values, "node", [(i, i ^ bits) for i in range(size)])


def paired_shards(
    moe_input,
    norm_gain,
    router_weight,
    routes,
    gate_weight,
    up_weight,
    down_weight,
    queries,
    key_cache,
    value_cache,
    new_keys,
    new_values,
    cache_lengths,
):
    rows, width = moe_input.shape
    capacity = rows // 2
    columns = lax.axis_size("node") // 4
    block = 2 * capacity
    half = columns * capacity
    named = routes.T
    gain = norm_gain

    def like(lines, dtype=BF16):
        return jax.ShapeDtypeStruct((lines, width), dtype)

    def held(lines, dtype=BF16):
        return pltpu.VMEM((lines, width), dtype)

    packed = call(
        functools.partial(pack_kernel, capacity),
        "pack",
        (like(block),) * columns,
        [pl.BlockSpec(memory_space=pltpu.HBM)] * 2,
        [pltpu.with_memory_space_constraint(array, pltpu.HBM) for array in (moe_input, named)],
        [
            pltpu.VMEM(moe_input.shape, BF16),
            pltpu.VMEM(named.shape, jnp.int32),
            pltpu.SemaphoreType.DMA((2,)),
        ],
        cost=pl.CostEstimate(flops=10**11, bytes_accessed=64 * MIB, transcendentals=0),
    )
    blocks = [packed[0]] + [exchange(packed[k], 4 * k) for k in range(1, columns)]
    attended, table = call(
        functools.partial(side_kernel, capacity),
        "side",
        (like(rows), jax.ShapeDtypeStruct((columns * block, rows), F32)),
        [pl.BlockSpec(memory_space=pltpu.SMEM), WHOLE, ANY, ANY] + [WHOLE] * 6,
        (
            cache_lengths,
            queries,
            key_cache,
            value_cache,
            new_keys,
            new_values,
            moe_input,
            gain,
            router_weight.T,
            named,
        ),
        [
            pltpu.VMEM(key_cache.shape, BF16),
            pltpu.VMEM(value_cache.shape, BF16),
            pltpu.SemaphoreType.DMA((2,)),
        ],
        cost=pl.CostEstimate(flops=10**8, bytes_accessed=4 * MIB, transcendentals=0),
    )
    keep, send = call(
        functools.partial(halves_kernel, capacity),
        "halves",
        (like(half),) * 2,
        [WHOLE] * columns + [ANY],
        (*blocks, table),
    )
    far_keep = exchange(keep, 1)
    across = exchange(send, 2)
    other_table = exchange(table, 2)
    far_across = exchange(across, 1)
    slots = 2
    lines = max(4 * half, 128)
    own, far = call(
        functools.partial(expert_kernel, slots),
        "expert",
        (held(2 * half, F32), held(2 * half)),
        [WHOLE] * 7 + [ANY],
        (
            *[
                pltpu.with_memory_space_constraint(part, pltpu.VMEM)
                for part in (keep, across, far_keep, far_across)
            ],
            gain,
            pltpu.with_memory_space_constraint(gate_weight, pltpu.VMEM),
            pltpu.with_memory_space_constraint(up_weight, pltpu.VMEM),
            down_weight,
        ),
        [
            pltpu.VMEM((lines, width), BF16),
            pltpu.VMEM((2, lines, TILE), BF16),
            pltpu.VMEM((4 * half, width), F32),
            pltpu.VMEM((slots, TILE, width), BF16),
            pltpu.SemaphoreType.DMA((slots,)),
        ],
        limit=12,
    )
    sums = call(
        functools.partial(merge_kernel, capacity),
        "merge",
        (like(block),) * columns,
        [WHOLE] * 2,
        (pltpu.with_memory_space_constraint(own, pltpu.VMEM), exchange(far, 1)),
    )
    results = [sums[0]] + [exchange(sums[k], 4 * k) for k in range(1, columns)]
    mine, theirs = call(
        functools.partial(mix_kernel, capacity),
        "mix",
        (held(rows, F32), like(rows)),
        [WHOLE] * (2 + columns),
        (table, other_table, *results),
    )
    moe_output = call(
        final_kernel,
        "final",
        like(rows),
        [WHOLE] * 2,
        (pltpu.with_memory_space_constraint(mine, pltpu.VMEM), exchange(theirs, 2)),
    )
    return moe_output, attended


def shards(*arrays):
    experts = arrays[2].shape[1]
    devices = lax.axis_size("node")
    units = arrays[4].shape[2]
    if devices == 2 * experts and devices % 8 == 0 and units % TILE == 0 and arrays[0].shape[0] == 8:
        return paired_shards(*arrays)
    return plain_shards(*arrays)


def solution(mesh):
    in_specs = (
        P(("groups", "node"), None),
        P(),
        P(),
        P(("groups", "node"), None),
        P("node", None, None),
        P("node", None, None),
        P("node", None, None),
        P(("groups", "node"), None),
        P(("groups", "node"), None, None),
        P(("groups", "node"), None, None),
        P(("groups", "node"), None),
        P(("groups", "node"), None),
        P(("groups", "node")),
    )
    out_specs = (P(("groups", "node"), None), P(("groups", "node"), None))
    return jax.shard_map(shards, mesh=mesh, in_specs=in_specs, out_specs=out_specs, check_vma=False)
```

```python
import functools

import jax
import jax.numpy as jnp
from jax import lax
from jax.experimental import pallas as pl
from jax.experimental.pallas import tpu as pltpu
from jax.sharding import PartitionSpec as P

HEADS = 24
KVH = 4
HD = 128
GROUP = 6
TILE = 512
MIB = 1 << 20
F32 = jnp.float32
BF16 = jnp.bfloat16
WHOLE = pl.BlockSpec(memory_space=pltpu.VMEM)
ANY = pl.BlockSpec(memory_space=pl.ANY)


def normalize(values, gain):
    wide = values.astype(jnp.float32)
    meansq = jnp.mean(wide * wide, axis=-1, keepdims=True)
    return (wide * lax.rsqrt(meansq + 1e-05) * gain.astype(jnp.float32)).astype(jnp.bfloat16)


def send_back(partial_rows, experts, slices):
    returned = lax.all_to_all(partial_rows, "node", split_axis=0, concat_axis=0, tiled=True)
    count = returned.shape[1]
    width = returned.shape[2]
    return jnp.sum(returned.reshape(experts, slices, count, width).astype(jnp.float32), axis=1)


def run_expert(received, gate_slice, up_slice, down_slice):
    senders, count, width = received.shape
    flat = received.reshape(senders * count, width)
    gate = jnp.dot(flat, gate_slice, preferred_element_type=jnp.float32)
    upper = jnp.dot(flat, up_slice, preferred_element_type=jnp.float32)
    hidden = (jax.nn.silu(gate) * upper).astype(jnp.bfloat16)
    part = jnp.dot(hidden, down_slice, preferred_element_type=jnp.float32).astype(jnp.bfloat16)
    return part.reshape(senders, count, width)


def plain_attention(queries, key_cache, value_cache, new_keys, new_values, cache_lengths):
    rows = queries.shape[0]
    length = key_cache.shape[1]
    scale = 1.0 / HD**0.5
    query = queries.reshape(rows, KVH, GROUP, HD)
    keys = key_cache.reshape(rows, length, KVH, HD)
    vals = value_cache.reshape(rows, length, KVH, HD)
    score = jnp.einsum("rkgh,rlkh->rkgl", query, keys, preferred_element_type=jnp.float32) * scale
    live = jnp.arange(length, dtype=jnp.int32)[None, :] < cache_lengths[:, None]
    score = jnp.where(live[:, None, None, :], score, -jnp.inf)
    own = (
        jnp.einsum(
            "rkgh,rkh->rkg",
            query,
            new_keys.reshape(rows, KVH, HD),
            preferred_element_type=jnp.float32,
        )
        * scale
    )
    top = jnp.maximum(jnp.max(score, axis=-1), own)
    weights = jnp.exp(score - top[..., None])
    own_weight = jnp.exp(own - top)
    total = jnp.sum(weights, axis=-1) + own_weight
    probs = (weights / total[..., None]).astype(jnp.bfloat16)
    own_prob = (own_weight / total).astype(jnp.bfloat16)
    mixed = jnp.einsum("rkgl,rlkh->rkgh", probs, vals, preferred_element_type=jnp.float32)
    mixed = mixed + own_prob.astype(jnp.float32)[..., None] * new_values.reshape(
        rows, KVH, 1, HD
    ).astype(jnp.float32)
    return mixed.reshape(rows, HEADS * HD).astype(jnp.bfloat16)


def plain_shards(
    moe_input,
    norm_gain,
    router_weight,
    routes,
    gate_weight,
    up_weight,
    down_weight,
    queries,
    key_cache,
    value_cache,
    new_keys,
    new_values,
    cache_lengths,
):
    rows, width = moe_input.shape
    experts = router_weight.shape[1]
    devices = lax.axis_size("node")
    slices = devices // experts
    capacity = rows // 2
    normed = normalize(moe_input, norm_gain)
    logits = jnp.dot(normed, router_weight, preferred_element_type=jnp.float32)
    onehot_int = (routes[:, :, None] == jnp.arange(experts, dtype=jnp.int32)[None, None, :]).astype(
        jnp.int32
    )
    onehot = onehot_int.astype(jnp.float32)
    picked = jnp.sum(onehot * logits[:, None, :], axis=-1)
    weight = 1.0 / (1.0 + jnp.exp(picked[:, ::-1] - picked))
    member_int = jnp.sum(onehot_int, axis=1)
    ranks_int = jnp.cumsum(member_int, axis=0) - member_int
    slots = jnp.arange(capacity, dtype=jnp.int32)
    select = (
        jnp.transpose(member_int)[:, None, :]
        * (jnp.transpose(ranks_int)[:, None, :] == slots[None, :, None]).astype(jnp.int32)
    ).astype(jnp.bfloat16)
    gate_slice = gate_weight[0]
    up_slice = up_weight[0]
    down_slice = down_weight[0]
    packed = jnp.einsum("ecr,rd->ecd", select, normed, preferred_element_type=jnp.float32).astype(
        jnp.bfloat16
    )
    outgoing = jnp.broadcast_to(packed[:, None], (experts, slices, capacity, width)).reshape(
        devices, capacity, width
    )
    summed = send_back(
        run_expert(
            lax.all_to_all(outgoing, "node", split_axis=0, concat_axis=0, tiled=True),
            gate_slice,
            up_slice,
            down_slice,
        ),
        experts,
        slices,
    )
    slot_of = jnp.sum(onehot_int * ranks_int[:, None, :], axis=-1)
    position = routes * capacity + slot_of
    picked_rows = summed.reshape(experts * capacity, width)[position]
    moe_output = jnp.sum(weight[:, :, None] * picked_rows, axis=1).astype(jnp.bfloat16)
    attention_output = plain_attention(
        queries, key_cache, value_cache, new_keys, new_values, cache_lengths
    )
    return (moe_output, attention_output)


def select_slots(routes, experts, capacity):
    lines, rows = experts.shape
    named = [routes[k : k + 1, :] == experts for k in range(2)]
    member = jnp.where(named[0] | named[1], 1.0, 0.0)
    before = lax.broadcasted_iota(jnp.int32, (rows, rows), 0) < lax.broadcasted_iota(
        jnp.int32, (rows, rows), 1
    )
    rank = jnp.dot(member, jnp.where(before, 1.0, 0.0), preferred_element_type=F32)
    slot = (lax.broadcasted_iota(jnp.int32, (lines, rows), 0) % capacity).astype(F32)
    return [flag & (rank == slot) for flag in named]


def line_experts(column, capacity, lines, rows):
    line = lax.broadcasted_iota(jnp.int32, (lines, rows), 0)
    block = 2 * capacity
    return ((line // block) ^ column) * 2 + (line % block) // capacity


def pack_kernel(capacity, x_hbm, routes_hbm, *refs):
    *out_refs, x_ref, routes_ref, sems = refs
    copies = [
        pltpu.make_async_copy(routes_hbm, routes_ref, sems.at[0]),
        pltpu.make_async_copy(x_hbm, x_ref, sems.at[1]),
    ]
    for copy in copies:
        copy.start()
    for copy in copies:
        copy.wait()
    column = lax.axis_index("node") // 4
    rows = x_ref.shape[0]
    block = out_refs[0].shape[0]
    lines = block * len(out_refs)
    first, second = select_slots(
        routes_ref[...], line_experts(column, capacity, lines, rows), capacity
    )
    chosen = jnp.where(first | second, 1.0, 0.0).astype(BF16)
    packed = jnp.dot(chosen, x_ref[...], preferred_element_type=F32)
    for k, out_ref in enumerate(out_refs):
        out_ref[...] = packed[k * block : (k + 1) * block].astype(BF16)


def far_first(columns):
    return sorted(range(columns), key=lambda k: (k < columns // 2, -k))


def back_order(columns):
    order = far_first(columns)
    return [order[0], order[2], order[1], *order[3:]]


def halves_kernel(capacity, *refs):
    *in_refs, _, keep_ref, send_ref = refs
    mine = (lax.axis_index("node") // 2) % 2
    block = 2 * capacity
    lines = len(in_refs) * block
    half = lines // 2
    out_line = lax.broadcasted_iota(jnp.int32, (lines, lines), 0)
    in_line = lax.broadcasted_iota(jnp.int32, (lines, lines), 1)
    which = jnp.where(out_line < half, mine, 1 - mine)
    within = out_line % half
    source = (within // capacity) * block + which * capacity + within % capacity
    move = jnp.where(in_line == source, 1.0, 0.0).astype(BF16)
    order = far_first(len(in_refs))
    values = jnp.concatenate([in_refs[order.index(k)][...] for k in range(len(order))], axis=0)
    moved = jnp.dot(move, values, preferred_element_type=F32)
    keep_ref[...] = moved[:half].astype(BF16)
    send_ref[...] = moved[half:].astype(BF16)


def merge_kernel(capacity, own_ref, far_ref, *out_refs):
    block = 2 * capacity
    lines = block * len(out_refs)
    out_line = lax.broadcasted_iota(jnp.int32, (lines, lines), 0)
    in_line = lax.broadcasted_iota(jnp.int32, (lines, lines), 1)
    which = (out_line % block) // capacity
    source = which * (lines // 2) + (out_line // block) * capacity + out_line % capacity
    move = jnp.where(in_line == source, 1.0, 0.0).astype(BF16)
    values = (own_ref[...] + far_ref[...].astype(F32)).astype(BF16)
    moved = jnp.dot(move, values, preferred_element_type=F32)
    for k, out_ref in enumerate(out_refs):
        out_ref[...] = moved[k * block : (k + 1) * block].astype(BF16)


def rms(values, gain):
    wide = values.astype(F32)
    meansq = jnp.mean(wide * wide, axis=-1, keepdims=True)
    return (wide * lax.rsqrt(meansq + 1e-05) * gain.astype(F32).reshape(1, -1)).astype(BF16)


def attention(lengths_ref, q_ref, k_ref, v_ref, nk_ref, nv_ref, out_ref):
    rows = q_ref.shape[0]
    length = k_ref.shape[1]
    groups = k_ref.shape[2] // HD
    per_group = q_ref.shape[1] // HD // groups
    lines, columns = per_group * rows, rows * length
    scale = 1.0 / HD**0.5
    row = lax.broadcasted_iota(jnp.int32, (lines, 1), 0) % rows
    count = jnp.zeros((lines, 1), jnp.int32)
    for r in range(rows):
        count = jnp.where(row == r, lengths_ref[r], count)
    position = lax.broadcasted_iota(jnp.int32, (lines, columns), 1) - row * length
    live = (position >= 0) & (position < count)
    for g in range(groups):
        lanes = slice(g * HD, (g + 1) * HD)
        heads = [slice(h * HD, (h + 1) * HD) for h in range(g * per_group, (g + 1) * per_group)]
        query = jnp.concatenate([q_ref[:, head].astype(F32) for head in heads], axis=0)
        keys = k_ref[:, :, lanes].reshape(columns, HD)
        values = v_ref[:, :, lanes].reshape(columns, HD)
        new_key = jnp.concatenate([nk_ref[:, lanes].astype(F32)] * per_group, axis=0)
        new_value = jnp.concatenate([nv_ref[:, lanes].astype(F32)] * per_group, axis=0)
        score = (
            lax.dot_general(
                query.astype(BF16), keys, (((1,), (1,)), ((), ())), preferred_element_type=F32
            )
            * scale
        )
        own = jnp.sum(query * new_key, axis=-1, keepdims=True) * scale
        score = jnp.where(live, score, -jnp.inf)
        top = jnp.maximum(jnp.max(score, axis=-1, keepdims=True), own)
        weights = jnp.exp(score - top)
        own_weight = jnp.exp(own - top)
        total = jnp.sum(weights, axis=-1, keepdims=True) + own_weight
        probs = (weights / total).astype(BF16)
        own_prob = (own_weight / total).astype(BF16).astype(F32)
        mixed = jnp.dot(probs, values, preferred_element_type=F32) + own_prob * new_value
        for j, head in enumerate(heads):
            out_ref[:, head] = mixed[j * rows : (j + 1) * rows].astype(BF16)


def side_kernel(
    capacity,
    lengths_ref,
    q_ref,
    k_hbm,
    v_hbm,
    nk_ref,
    nv_ref,
    x_ref,
    gain_ref,
    router_ref,
    routes_ref,
    out_ref,
    table_ref,
    k_ref,
    v_ref,
    sems,
):
    copies = [
        pltpu.make_async_copy(k_hbm, k_ref, sems.at[0]),
        pltpu.make_async_copy(v_hbm, v_ref, sems.at[1]),
    ]
    for copy in copies:
        copy.start()
    logits = lax.dot_general(
        router_ref[...],
        rms(x_ref[...], gain_ref[...]),
        (((1,), (1,)), ((), ())),
        preferred_element_type=F32,
    )
    table_ref[...] = slot_weights(capacity, routes_ref[...], logits, table_ref.shape[0])
    for copy in copies:
        copy.wait()
    attention(lengths_ref, q_ref, k_ref, v_ref, nk_ref, nv_ref, out_ref)


def down_copy(down_ref, buf, sems, tile, slot):
    return pltpu.make_async_copy(
        down_ref.at[0, pl.ds(pl.multiple_of(tile * TILE, TILE), TILE), :],
        buf.at[slot],
        sems.at[slot],
    )


def expert_kernel(
    slots,
    a_ref,
    b_ref,
    c_ref,
    d_ref,
    gain_ref,
    gate_ref,
    up_ref,
    down_ref,
    own_ref,
    far_ref,
    x_buf,
    hidden,
    total,
    down_buf,
    sems,
):
    tiles = gate_ref.shape[2] // TILE
    part = a_ref.shape[0]
    lines = total.shape[0]
    for tile in range(min(slots, tiles)):
        down_copy(down_ref, down_buf, sems, tile, tile).start()
    for i, ref in enumerate((a_ref, b_ref, c_ref, d_ref)):
        x_buf[i * part : (i + 1) * part, :] = rms(ref[...], gain_ref[...])
    x_buf[lines:, :] = jnp.zeros_like(x_buf[lines:, :])
    total[...] = jnp.zeros_like(total)

    def activate(tile):
        cols = pl.ds(pl.multiple_of(tile * TILE, TILE), TILE)
        x = x_buf[...]
        gated = jnp.dot(x, gate_ref[0, :, cols], preferred_element_type=F32)
        upper = jnp.dot(x, up_ref[0, :, cols], preferred_element_type=F32)
        return (gated / (1.0 + jnp.exp(-gated)) * upper).astype(BF16)

    def project(tile):
        slot = lax.rem(tile, slots)
        down_copy(down_ref, down_buf, sems, tile, slot).wait()
        return jnp.dot(hidden[lax.rem(tile, 2)], down_buf[slot], preferred_element_type=F32)

    def refill(tile):
        @pl.when(tile + slots < tiles)
        def _():
            down_copy(down_ref, down_buf, sems, tile + slots, lax.rem(tile, slots)).start()

    hidden[0] = activate(0)

    def step(tile, carry):
        product = project(tile - 1)
        hidden[lax.rem(tile, 2)] = activate(tile)
        total[...] += product[:lines]
        refill(tile - 1)
        return carry

    lax.fori_loop(1, tiles, step, 0)
    result = total[...] + project(tiles - 1)[:lines]
    own_ref[...] = result[: 2 * part]
    far_ref[...] = result[2 * part :].astype(BF16)


def slot_weights(capacity, routes, logits, lines):
    column, mine = lax.axis_index("node") // 4, (lax.axis_index("node") // 2) % 2
    shape = (lines, routes.shape[1])
    line = lax.broadcasted_iota(jnp.int32, shape, 0)
    block = 2 * capacity
    which = (line % block) // capacity
    experts = ((line // block) ^ column) * 2 + jnp.where(which == 0, mine, 1 - mine)
    expert = lax.broadcasted_iota(jnp.int32, logits.shape, 0)
    picked = [
        jnp.sum(jnp.where(routes[k : k + 1, :] == expert, logits, 0.0), axis=0, keepdims=True)
        for k in range(2)
    ]
    hits = select_slots(routes, experts, capacity)
    table = jnp.zeros(shape, F32)
    for k in range(2):
        weight = 1.0 / (1.0 + jnp.exp(picked[1 - k] - picked[k]))
        table += jnp.where(hits[k], weight, 0.0)
    return table


def mix_kernel(capacity, table_ref, other_ref, *refs):
    *in_refs, own_ref, send_ref = refs
    which = lax.broadcasted_iota(jnp.int32, table_ref.shape, 0) % (2 * capacity) // capacity
    table = jnp.concatenate(
        [
            jnp.where(which == 0, table_ref[...], 0.0),
            jnp.where(which == 1, other_ref[...], 0.0),
        ],
        axis=1,
    )
    high = table.astype(BF16)
    rest = table - high.astype(F32)
    middle = rest.astype(BF16)
    low = (rest - middle.astype(F32)).astype(BF16)
    order = back_order(len(in_refs))
    values = jnp.concatenate([in_refs[order.index(k)][...] for k in range(len(order))], axis=0)
    terms = [
        lax.dot_general(term, values, (((0,), (0,)), ((), ())), preferred_element_type=F32)
        for term in (low, middle, high)
    ]
    mixed = terms[0] + terms[1] + terms[2]
    rows = own_ref.shape[0]
    own_ref[...] = mixed[:rows]
    send_ref[...] = mixed[rows:].astype(BF16)


def final_kernel(own_ref, other_ref, out_ref):
    out_ref[...] = (own_ref[...] + other_ref[...].astype(F32)).astype(BF16)


def call(kernel, name, outs, ins, operands, scratch=(), limit=4, cost=None):
    return pl.pallas_call(
        kernel,
        out_shape=outs,
        in_specs=ins,
        out_specs=tuple(WHOLE for _ in outs) if isinstance(outs, tuple) else WHOLE,
        scratch_shapes=list(scratch),
        compiler_params=pltpu.CompilerParams(vmem_limit_bytes=limit * MIB),
        cost_estimate=cost,
        name=name,
    )(*operands)


def exchange(values, bits):
    size = lax.axis_size("node")
    return lax.ppermute(values, "node", [(i, i ^ bits) for i in range(size)])


def paired_shards(
    moe_input,
    norm_gain,
    router_weight,
    routes,
    gate_weight,
    up_weight,
    down_weight,
    queries,
    key_cache,
    value_cache,
    new_keys,
    new_values,
    cache_lengths,
):
    rows, width = moe_input.shape
    capacity = rows // 2
    columns = lax.axis_size("node") // 4
    block = 2 * capacity
    half = columns * capacity
    named = routes.T
    gain = norm_gain

    def like(lines, dtype=BF16):
        return jax.ShapeDtypeStruct((lines, width), dtype)

    def held(lines, dtype=BF16):
        return pltpu.VMEM((lines, width), dtype)

    packed = call(
        functools.partial(pack_kernel, capacity),
        "pack",
        (like(block),) * columns,
        [pl.BlockSpec(memory_space=pltpu.HBM)] * 2,
        [pltpu.with_memory_space_constraint(array, pltpu.HBM) for array in (moe_input, named)],
        [
            pltpu.VMEM(moe_input.shape, BF16),
            pltpu.VMEM(named.shape, jnp.int32),
            pltpu.SemaphoreType.DMA((2,)),
        ],
        cost=pl.CostEstimate(flops=10**11, bytes_accessed=64 * MIB, transcendentals=0),
    )
    blocks = [exchange(packed[k], 4 * k) if k else packed[k] for k in far_first(columns)]
    attended, table = call(
        functools.partial(side_kernel, capacity),
        "side",
        (like(rows), jax.ShapeDtypeStruct((columns * block, rows), F32)),
        [pl.BlockSpec(memory_space=pltpu.SMEM), WHOLE, ANY, ANY] + [WHOLE] * 6,
        (
            cache_lengths,
            queries,
            key_cache,
            value_cache,
            new_keys,
            new_values,
            moe_input,
            gain,
            router_weight.T,
            named,
        ),
        [
            pltpu.VMEM(key_cache.shape, BF16),
            pltpu.VMEM(value_cache.shape, BF16),
            pltpu.SemaphoreType.DMA((2,)),
        ],
        cost=pl.CostEstimate(flops=10**8, bytes_accessed=4 * MIB, transcendentals=0),
    )
    keep, send = call(
        functools.partial(halves_kernel, capacity),
        "halves",
        (like(half),) * 2,
        [WHOLE] * columns + [ANY],
        (*blocks, table),
    )
    far_keep = exchange(keep, 1)
    across = exchange(send, 2)
    other_table = exchange(table, 2)
    far_across = exchange(across, 1)
    slots = 2
    lines = max(4 * half, 128)
    own, far = call(
        functools.partial(expert_kernel, slots),
        "expert",
        (held(2 * half, F32), held(2 * half)),
        [WHOLE] * 7 + [ANY],
        (
            *[
                pltpu.with_memory_space_constraint(part, pltpu.VMEM)
                for part in (keep, across, far_keep, far_across)
            ],
            gain,
            pltpu.with_memory_space_constraint(gate_weight, pltpu.VMEM),
            pltpu.with_memory_space_constraint(up_weight, pltpu.VMEM),
            down_weight,
        ),
        [
            pltpu.VMEM((lines, width), BF16),
            pltpu.VMEM((2, lines, TILE), BF16),
            pltpu.VMEM((4 * half, width), F32),
            pltpu.VMEM((slots, TILE, width), BF16),
            pltpu.SemaphoreType.DMA((slots,)),
        ],
        limit=12,
    )
    sums = call(
        functools.partial(merge_kernel, capacity),
        "merge",
        (like(block),) * columns,
        [WHOLE] * 2,
        (pltpu.with_memory_space_constraint(own, pltpu.VMEM), exchange(far, 1)),
    )
    results = [exchange(sums[k], 4 * k) if k else sums[k] for k in back_order(columns)]
    mine, theirs = call(
        functools.partial(mix_kernel, capacity),
        "mix",
        (held(rows, F32), like(rows)),
        [WHOLE] * (2 + columns),
        (table, other_table, *results),
    )
    moe_output = call(
        final_kernel,
        "final",
        like(rows),
        [WHOLE] * 2,
        (pltpu.with_memory_space_constraint(mine, pltpu.VMEM), exchange(theirs, 2)),
    )
    return moe_output, attended


def shards(*arrays):
    experts = arrays[2].shape[1]
    devices = lax.axis_size("node")
    units = arrays[4].shape[2]
    if devices == 2 * experts and devices % 16 == 0 and units % TILE == 0 and arrays[0].shape[0] == 8:
        return paired_shards(*arrays)
    return plain_shards(*arrays)


def solution(mesh):
    in_specs = (
        P(("groups", "node"), None),
        P(),
        P(),
        P(("groups", "node"), None),
        P("node", None, None),
        P("node", None, None),
        P("node", None, None),
        P(("groups", "node"), None),
        P(("groups", "node"), None, None),
        P(("groups", "node"), None, None),
        P(("groups", "node"), None),
        P(("groups", "node"), None),
        P(("groups", "node")),
    )
    out_specs = (P(("groups", "node"), None), P(("groups", "node"), None))
    return jax.shard_map(shards, mesh=mesh, in_specs=in_specs, out_specs=out_specs, check_vma=False)
```

```python
import functools

import jax
import jax.numpy as jnp
from jax import lax
from jax.experimental import pallas as pl
from jax.experimental.pallas import tpu as pltpu
from jax.sharding import PartitionSpec as P

HEADS = 24
KVH = 4
HD = 128
GROUP = 6
TILE = 512
MIB = 1 << 20
F32 = jnp.float32
BF16 = jnp.bfloat16
WHOLE = pl.BlockSpec(memory_space=pltpu.VMEM)
ANY = pl.BlockSpec(memory_space=pl.ANY)


def normalize(values, gain):
    wide = values.astype(jnp.float32)
    meansq = jnp.mean(wide * wide, axis=-1, keepdims=True)
    return (wide * lax.rsqrt(meansq + 1e-05) * gain.astype(jnp.float32)).astype(jnp.bfloat16)


def send_back(partial_rows, experts, slices):
    returned = lax.all_to_all(partial_rows, "node", split_axis=0, concat_axis=0, tiled=True)
    count = returned.shape[1]
    width = returned.shape[2]
    return jnp.sum(returned.reshape(experts, slices, count, width).astype(jnp.float32), axis=1)


def run_expert(received, gate_slice, up_slice, down_slice):
    senders, count, width = received.shape
    flat = received.reshape(senders * count, width)
    gate = jnp.dot(flat, gate_slice, preferred_element_type=jnp.float32)
    upper = jnp.dot(flat, up_slice, preferred_element_type=jnp.float32)
    hidden = (jax.nn.silu(gate) * upper).astype(jnp.bfloat16)
    part = jnp.dot(hidden, down_slice, preferred_element_type=jnp.float32).astype(jnp.bfloat16)
    return part.reshape(senders, count, width)


def plain_attention(queries, key_cache, value_cache, new_keys, new_values, cache_lengths):
    rows = queries.shape[0]
    length = key_cache.shape[1]
    scale = 1.0 / HD**0.5
    query = queries.reshape(rows, KVH, GROUP, HD)
    keys = key_cache.reshape(rows, length, KVH, HD)
    vals = value_cache.reshape(rows, length, KVH, HD)
    score = jnp.einsum("rkgh,rlkh->rkgl", query, keys, preferred_element_type=jnp.float32) * scale
    live = jnp.arange(length, dtype=jnp.int32)[None, :] < cache_lengths[:, None]
    score = jnp.where(live[:, None, None, :], score, -jnp.inf)
    own = (
        jnp.einsum(
            "rkgh,rkh->rkg",
            query,
            new_keys.reshape(rows, KVH, HD),
            preferred_element_type=jnp.float32,
        )
        * scale
    )
    top = jnp.maximum(jnp.max(score, axis=-1), own)
    weights = jnp.exp(score - top[..., None])
    own_weight = jnp.exp(own - top)
    total = jnp.sum(weights, axis=-1) + own_weight
    probs = (weights / total[..., None]).astype(jnp.bfloat16)
    own_prob = (own_weight / total).astype(jnp.bfloat16)
    mixed = jnp.einsum("rkgl,rlkh->rkgh", probs, vals, preferred_element_type=jnp.float32)
    mixed = mixed + own_prob.astype(jnp.float32)[..., None] * new_values.reshape(
        rows, KVH, 1, HD
    ).astype(jnp.float32)
    return mixed.reshape(rows, HEADS * HD).astype(jnp.bfloat16)


def plain_shards(
    moe_input,
    norm_gain,
    router_weight,
    routes,
    gate_weight,
    up_weight,
    down_weight,
    queries,
    key_cache,
    value_cache,
    new_keys,
    new_values,
    cache_lengths,
):
    rows, width = moe_input.shape
    experts = router_weight.shape[1]
    devices = lax.axis_size("node")
    slices = devices // experts
    capacity = rows // 2
    normed = normalize(moe_input, norm_gain)
    logits = jnp.dot(normed, router_weight, preferred_element_type=jnp.float32)
    onehot_int = (routes[:, :, None] == jnp.arange(experts, dtype=jnp.int32)[None, None, :]).astype(
        jnp.int32
    )
    onehot = onehot_int.astype(jnp.float32)
    picked = jnp.sum(onehot * logits[:, None, :], axis=-1)
    weight = 1.0 / (1.0 + jnp.exp(picked[:, ::-1] - picked))
    member_int = jnp.sum(onehot_int, axis=1)
    ranks_int = jnp.cumsum(member_int, axis=0) - member_int
    slots = jnp.arange(capacity, dtype=jnp.int32)
    select = (
        jnp.transpose(member_int)[:, None, :]
        * (jnp.transpose(ranks_int)[:, None, :] == slots[None, :, None]).astype(jnp.int32)
    ).astype(jnp.bfloat16)
    gate_slice = gate_weight[0]
    up_slice = up_weight[0]
    down_slice = down_weight[0]
    packed = jnp.einsum("ecr,rd->ecd", select, normed, preferred_element_type=jnp.float32).astype(
        jnp.bfloat16
    )
    outgoing = jnp.broadcast_to(packed[:, None], (experts, slices, capacity, width)).reshape(
        devices, capacity, width
    )
    summed = send_back(
        run_expert(
            lax.all_to_all(outgoing, "node", split_axis=0, concat_axis=0, tiled=True),
            gate_slice,
            up_slice,
            down_slice,
        ),
        experts,
        slices,
    )
    slot_of = jnp.sum(onehot_int * ranks_int[:, None, :], axis=-1)
    position = routes * capacity + slot_of
    picked_rows = summed.reshape(experts * capacity, width)[position]
    moe_output = jnp.sum(weight[:, :, None] * picked_rows, axis=1).astype(jnp.bfloat16)
    attention_output = plain_attention(
        queries, key_cache, value_cache, new_keys, new_values, cache_lengths
    )
    return (moe_output, attention_output)


def select_slots(routes, experts, capacity):
    lines, rows = experts.shape
    named = [routes[k : k + 1, :] == experts for k in range(2)]
    member = jnp.where(named[0] | named[1], 1.0, 0.0)
    before = lax.broadcasted_iota(jnp.int32, (rows, rows), 0) < lax.broadcasted_iota(
        jnp.int32, (rows, rows), 1
    )
    rank = jnp.dot(member, jnp.where(before, 1.0, 0.0), preferred_element_type=F32)
    slot = (lax.broadcasted_iota(jnp.int32, (lines, rows), 0) % capacity).astype(F32)
    return [flag & (rank == slot) for flag in named]


def line_experts(column, capacity, lines, rows):
    line = lax.broadcasted_iota(jnp.int32, (lines, rows), 0)
    block = 2 * capacity
    return ((line // block) ^ column) * 2 + (line % block) // capacity


def pack_kernel(capacity, x_hbm, routes_hbm, *refs):
    *out_refs, x_ref, routes_ref, sems = refs
    copies = [
        pltpu.make_async_copy(routes_hbm, routes_ref, sems.at[0]),
        pltpu.make_async_copy(x_hbm, x_ref, sems.at[1]),
    ]
    for copy in copies:
        copy.start()
    for copy in copies:
        copy.wait()
    column = lax.axis_index("node") // 4
    rows = x_ref.shape[0]
    block = out_refs[0].shape[0]
    lines = block * len(out_refs)
    first, second = select_slots(
        routes_ref[...], line_experts(column, capacity, lines, rows), capacity
    )
    chosen = jnp.where(first | second, 1.0, 0.0).astype(BF16)
    packed = jnp.dot(chosen, x_ref[...], preferred_element_type=F32)
    for k, out_ref in enumerate(out_refs):
        out_ref[...] = packed[k * block : (k + 1) * block].astype(BF16)


def far_first(columns):
    return sorted(range(columns), key=lambda k: (k < columns // 2, -k))


def back_order(columns):
    order = far_first(columns)
    return [order[0], order[2], order[1], *order[3:]]


def halves_kernel(capacity, *refs):
    *in_refs, _, keep_ref, send_ref = refs
    mine = (lax.axis_index("node") // 2) % 2
    block = 2 * capacity
    lines = len(in_refs) * block
    half = lines // 2
    out_line = lax.broadcasted_iota(jnp.int32, (lines, lines), 0)
    in_line = lax.broadcasted_iota(jnp.int32, (lines, lines), 1)
    which = jnp.where(out_line < half, mine, 1 - mine)
    within = out_line % half
    source = (within // capacity) * block + which * capacity + within % capacity
    move = jnp.where(in_line == source, 1.0, 0.0).astype(BF16)
    order = far_first(len(in_refs))
    values = jnp.concatenate([in_refs[order.index(k)][...] for k in range(len(order))], axis=0)
    moved = jnp.dot(move, values, preferred_element_type=F32)
    keep_ref[...] = moved[:half].astype(BF16)
    send_ref[...] = moved[half:].astype(BF16)


def merge_kernel(capacity, own_ref, far_ref, *out_refs):
    block = 2 * capacity
    lines = block * len(out_refs)
    out_line = lax.broadcasted_iota(jnp.int32, (lines, lines), 0)
    in_line = lax.broadcasted_iota(jnp.int32, (lines, lines), 1)
    which = (out_line % block) // capacity
    source = which * (lines // 2) + (out_line // block) * capacity + out_line % capacity
    move = jnp.where(in_line == source, 1.0, 0.0).astype(BF16)
    values = (own_ref[...] + far_ref[...].astype(F32)).astype(BF16)
    moved = jnp.dot(move, values, preferred_element_type=F32)
    for k, out_ref in enumerate(out_refs):
        out_ref[...] = moved[k * block : (k + 1) * block].astype(BF16)


def rms(values, gain):
    wide = values.astype(F32)
    meansq = jnp.mean(wide * wide, axis=-1, keepdims=True)
    return (wide * lax.rsqrt(meansq + 1e-05) * gain.astype(F32).reshape(1, -1)).astype(BF16)


def attention(lengths_ref, q_ref, k_ref, v_ref, nk_ref, nv_ref, out_ref):
    rows = q_ref.shape[0]
    length = k_ref.shape[1]
    groups = k_ref.shape[2] // HD
    per_group = q_ref.shape[1] // HD // groups
    lines, columns = per_group * rows, rows * length
    scale = 1.0 / HD**0.5
    row = lax.broadcasted_iota(jnp.int32, (lines, 1), 0) % rows
    count = jnp.zeros((lines, 1), jnp.int32)
    for r in range(rows):
        count = jnp.where(row == r, lengths_ref[r], count)
    position = lax.broadcasted_iota(jnp.int32, (lines, columns), 1) - row * length
    live = (position >= 0) & (position < count)
    for g in range(groups):
        lanes = slice(g * HD, (g + 1) * HD)
        heads = [slice(h * HD, (h + 1) * HD) for h in range(g * per_group, (g + 1) * per_group)]
        query = jnp.concatenate([q_ref[:, head].astype(F32) for head in heads], axis=0)
        keys = k_ref[:, :, lanes].reshape(columns, HD)
        values = v_ref[:, :, lanes].reshape(columns, HD)
        new_key = jnp.concatenate([nk_ref[:, lanes].astype(F32)] * per_group, axis=0)
        new_value = jnp.concatenate([nv_ref[:, lanes].astype(F32)] * per_group, axis=0)
        score = (
            lax.dot_general(
                query.astype(BF16), keys, (((1,), (1,)), ((), ())), preferred_element_type=F32
            )
            * scale
        )
        own = jnp.sum(query * new_key, axis=-1, keepdims=True) * scale
        score = jnp.where(live, score, -jnp.inf)
        top = jnp.maximum(jnp.max(score, axis=-1, keepdims=True), own)
        weights = jnp.exp(score - top)
        own_weight = jnp.exp(own - top)
        total = jnp.sum(weights, axis=-1, keepdims=True) + own_weight
        probs = (weights / total).astype(BF16)
        own_prob = (own_weight / total).astype(BF16).astype(F32)
        mixed = jnp.dot(probs, values, preferred_element_type=F32) + own_prob * new_value
        for j, head in enumerate(heads):
            out_ref[:, head] = mixed[j * rows : (j + 1) * rows].astype(BF16)


def attend_kernel(lengths_ref, q_ref, k_ref, v_ref, nk_ref, nv_ref, _, out_ref):
    attention(lengths_ref, q_ref, k_ref, v_ref, nk_ref, nv_ref, out_ref)


def weigh_kernel(capacity, x_ref, gain_ref, router_ref, routes_ref, table_ref):
    logits = lax.dot_general(
        router_ref[...],
        rms(x_ref[...], gain_ref[...]),
        (((1,), (1,)), ((), ())),
        preferred_element_type=F32,
    )
    table_ref[...] = slot_weights(capacity, routes_ref[...], logits, table_ref.shape[0])


def down_copy(down_ref, buf, sems, tile, slot):
    return pltpu.make_async_copy(
        down_ref.at[0, pl.ds(pl.multiple_of(tile * TILE, TILE), TILE), :],
        buf.at[slot],
        sems.at[slot],
    )


def expert_kernel(
    slots,
    a_ref,
    b_ref,
    c_ref,
    d_ref,
    gain_ref,
    gate_ref,
    up_ref,
    down_ref,
    own_ref,
    far_ref,
    x_buf,
    hidden,
    total,
    down_buf,
    sems,
):
    tiles = gate_ref.shape[2] // TILE
    part = a_ref.shape[0]
    lines = total.shape[0]
    for tile in range(min(slots, tiles)):
        down_copy(down_ref, down_buf, sems, tile, tile).start()
    for i, ref in enumerate((a_ref, b_ref, c_ref, d_ref)):
        x_buf[i * part : (i + 1) * part, :] = rms(ref[...], gain_ref[...])
    x_buf[lines:, :] = jnp.zeros_like(x_buf[lines:, :])
    total[...] = jnp.zeros_like(total)

    def activate(tile):
        cols = pl.ds(pl.multiple_of(tile * TILE, TILE), TILE)
        x = x_buf[...]
        gated = jnp.dot(x, gate_ref[0, :, cols], preferred_element_type=F32)
        upper = jnp.dot(x, up_ref[0, :, cols], preferred_element_type=F32)
        return (gated / (1.0 + jnp.exp(-gated)) * upper).astype(BF16)

    def project(tile):
        slot = lax.rem(tile, slots)
        down_copy(down_ref, down_buf, sems, tile, slot).wait()
        return jnp.dot(hidden[lax.rem(tile, 2)], down_buf[slot], preferred_element_type=F32)

    def refill(tile):
        @pl.when(tile + slots < tiles)
        def _():
            down_copy(down_ref, down_buf, sems, tile + slots, lax.rem(tile, slots)).start()

    hidden[0] = activate(0)

    def step(tile, carry):
        product = project(tile - 1)
        hidden[lax.rem(tile, 2)] = activate(tile)
        total[...] += product[:lines]
        refill(tile - 1)
        return carry

    lax.fori_loop(1, tiles, step, 0)
    result = total[...] + project(tiles - 1)[:lines]
    own_ref[...] = result[: 2 * part]
    far_ref[...] = result[2 * part :].astype(BF16)


def slot_weights(capacity, routes, logits, lines):
    column, mine = lax.axis_index("node") // 4, (lax.axis_index("node") // 2) % 2
    shape = (lines, routes.shape[1])
    line = lax.broadcasted_iota(jnp.int32, shape, 0)
    block = 2 * capacity
    which = (line % block) // capacity
    experts = ((line // block) ^ column) * 2 + jnp.where(which == 0, mine, 1 - mine)
    expert = lax.broadcasted_iota(jnp.int32, logits.shape, 0)
    picked = [
        jnp.sum(jnp.where(routes[k : k + 1, :] == expert, logits, 0.0), axis=0, keepdims=True)
        for k in range(2)
    ]
    hits = select_slots(routes, experts, capacity)
    table = jnp.zeros(shape, F32)
    for k in range(2):
        weight = 1.0 / (1.0 + jnp.exp(picked[1 - k] - picked[k]))
        table += jnp.where(hits[k], weight, 0.0)
    return table


def mix_kernel(capacity, table_ref, other_ref, *refs):
    *in_refs, own_ref, send_ref = refs
    which = lax.broadcasted_iota(jnp.int32, table_ref.shape, 0) % (2 * capacity) // capacity
    table = jnp.concatenate(
        [
            jnp.where(which == 0, table_ref[...], 0.0),
            jnp.where(which == 1, other_ref[...], 0.0),
        ],
        axis=1,
    )
    high = table.astype(BF16)
    rest = table - high.astype(F32)
    middle = rest.astype(BF16)
    low = (rest - middle.astype(F32)).astype(BF16)
    order = back_order(len(in_refs))
    values = jnp.concatenate([in_refs[order.index(k)][...] for k in range(len(order))], axis=0)
    terms = [
        lax.dot_general(term, values, (((0,), (0,)), ((), ())), preferred_element_type=F32)
        for term in (low, middle, high)
    ]
    mixed = terms[0] + terms[1] + terms[2]
    rows = own_ref.shape[0]
    own_ref[...] = mixed[:rows]
    send_ref[...] = mixed[rows:].astype(BF16)


def final_kernel(own_ref, other_ref, _, out_ref):
    out_ref[...] = (own_ref[...] + other_ref[...].astype(F32)).astype(BF16)


def call(kernel, name, outs, ins, operands, scratch=(), limit=4, cost=None):
    return pl.pallas_call(
        kernel,
        out_shape=outs,
        in_specs=ins,
        out_specs=tuple(WHOLE for _ in outs) if isinstance(outs, tuple) else WHOLE,
        scratch_shapes=list(scratch),
        compiler_params=pltpu.CompilerParams(vmem_limit_bytes=limit * MIB),
        cost_estimate=cost,
        name=name,
    )(*operands)


def exchange(values, bits):
    size = lax.axis_size("node")
    return lax.ppermute(values, "node", [(i, i ^ bits) for i in range(size)])


def paired_shards(
    moe_input,
    norm_gain,
    router_weight,
    routes,
    gate_weight,
    up_weight,
    down_weight,
    queries,
    key_cache,
    value_cache,
    new_keys,
    new_values,
    cache_lengths,
):
    rows, width = moe_input.shape
    capacity = rows // 2
    columns = lax.axis_size("node") // 4
    block = 2 * capacity
    half = columns * capacity
    named = routes.T
    gain = norm_gain

    def like(lines, dtype=BF16):
        return jax.ShapeDtypeStruct((lines, width), dtype)

    def held(lines, dtype=BF16):
        return pltpu.VMEM((lines, width), dtype)

    packed = call(
        functools.partial(pack_kernel, capacity),
        "pack",
        (like(block),) * columns,
        [pl.BlockSpec(memory_space=pltpu.HBM)] * 2,
        [pltpu.with_memory_space_constraint(array, pltpu.HBM) for array in (moe_input, named)],
        [
            pltpu.VMEM(moe_input.shape, BF16),
            pltpu.VMEM(named.shape, jnp.int32),
            pltpu.SemaphoreType.DMA((2,)),
        ],
        cost=pl.CostEstimate(flops=10**11, bytes_accessed=64 * MIB, transcendentals=0),
    )
    blocks = [exchange(packed[k], 4 * k) if k else packed[k] for k in far_first(columns)]
    (table,) = call(
        functools.partial(weigh_kernel, capacity),
        "weigh",
        (jax.ShapeDtypeStruct((columns * block, rows), F32),),
        [WHOLE] * 4,
        (moe_input, gain, router_weight.T, named),
    )
    keep, send = call(
        functools.partial(halves_kernel, capacity),
        "halves",
        (like(half),) * 2,
        [WHOLE] * columns + [ANY],
        (*blocks, table),
    )
    far_keep = exchange(keep, 1)
    across = exchange(send, 2)
    other_table = exchange(table, 2)
    far_across = exchange(across, 1)
    slots = 2
    lines = max(4 * half, 128)
    own, far = call(
        functools.partial(expert_kernel, slots),
        "expert",
        (held(2 * half, F32), held(2 * half)),
        [WHOLE] * 7 + [ANY],
        (
            *[
                pltpu.with_memory_space_constraint(part, pltpu.VMEM)
                for part in (keep, across, far_keep, far_across)
            ],
            gain,
            pltpu.with_memory_space_constraint(gate_weight, pltpu.VMEM),
            pltpu.with_memory_space_constraint(up_weight, pltpu.VMEM),
            down_weight,
        ),
        [
            pltpu.VMEM((lines, width), BF16),
            pltpu.VMEM((2, lines, TILE), BF16),
            pltpu.VMEM((4 * half, width), F32),
            pltpu.VMEM((slots, TILE, width), BF16),
            pltpu.SemaphoreType.DMA((slots,)),
        ],
        limit=12,
    )
    sums = call(
        functools.partial(merge_kernel, capacity),
        "merge",
        (like(block),) * columns,
        [WHOLE] * 2,
        (pltpu.with_memory_space_constraint(own, pltpu.VMEM), exchange(far, 1)),
    )
    results = [exchange(sums[k], 4 * k) if k else sums[k] for k in back_order(columns)]
    mine, theirs = call(
        functools.partial(mix_kernel, capacity),
        "mix",
        (held(rows, F32), like(rows)),
        [WHOLE] * (2 + columns),
        (table, other_table, *results),
    )
    (attended,) = call(
        attend_kernel,
        "attend",
        (pltpu.HBM((rows, width), BF16),),
        [pl.BlockSpec(memory_space=pltpu.SMEM)] + [WHOLE] * 5 + [ANY],
        (cache_lengths, queries, key_cache, value_cache, new_keys, new_values, theirs),
        cost=pl.CostEstimate(flops=10**8, bytes_accessed=4 * MIB, transcendentals=0),
    )
    moe_output = call(
        final_kernel,
        "final",
        like(rows),
        [WHOLE] * 2 + [pl.BlockSpec(memory_space=pltpu.HBM)],
        (
            pltpu.with_memory_space_constraint(mine, pltpu.VMEM),
            exchange(theirs, 2),
            pltpu.with_memory_space_constraint(attended, pltpu.HBM),
        ),
    )
    return moe_output, attended


def shards(*arrays):
    experts = arrays[2].shape[1]
    devices = lax.axis_size("node")
    units = arrays[4].shape[2]
    if devices == 2 * experts and devices % 16 == 0 and units % TILE == 0 and arrays[0].shape[0] == 8:
        return paired_shards(*arrays)
    return plain_shards(*arrays)


def solution(mesh):
    in_specs = (
        P(("groups", "node"), None),
        P(),
        P(),
        P(("groups", "node"), None),
        P("node", None, None),
        P("node", None, None),
        P("node", None, None),
        P(("groups", "node"), None),
        P(("groups", "node"), None, None),
        P(("groups", "node"), None, None),
        P(("groups", "node"), None),
        P(("groups", "node"), None),
        P(("groups", "node")),
    )
    out_specs = (P(("groups", "node"), None), P(("groups", "node"), None))
    return jax.shard_map(shards, mesh=mesh, in_specs=in_specs, out_specs=out_specs, check_vma=False)
```

```python
import functools

import jax
import jax.numpy as jnp
from jax import lax
from jax.experimental import pallas as pl
from jax.experimental.pallas import tpu as pltpu
from jax.sharding import PartitionSpec as P

HEADS = 24
KVH = 4
HD = 128
GROUP = 6
TILE = 512
MIB = 1 << 20
F32 = jnp.float32
BF16 = jnp.bfloat16
WHOLE = pl.BlockSpec(memory_space=pltpu.VMEM)
ANY = pl.BlockSpec(memory_space=pl.ANY)


def normalize(values, gain):
    wide = values.astype(jnp.float32)
    meansq = jnp.mean(wide * wide, axis=-1, keepdims=True)
    return (wide * lax.rsqrt(meansq + 1e-05) * gain.astype(jnp.float32)).astype(jnp.bfloat16)


def send_back(partial_rows, experts, slices):
    returned = lax.all_to_all(partial_rows, "node", split_axis=0, concat_axis=0, tiled=True)
    count = returned.shape[1]
    width = returned.shape[2]
    return jnp.sum(returned.reshape(experts, slices, count, width).astype(jnp.float32), axis=1)


def run_expert(received, gate_slice, up_slice, down_slice):
    senders, count, width = received.shape
    flat = received.reshape(senders * count, width)
    gate = jnp.dot(flat, gate_slice, preferred_element_type=jnp.float32)
    upper = jnp.dot(flat, up_slice, preferred_element_type=jnp.float32)
    hidden = (jax.nn.silu(gate) * upper).astype(jnp.bfloat16)
    part = jnp.dot(hidden, down_slice, preferred_element_type=jnp.float32).astype(jnp.bfloat16)
    return part.reshape(senders, count, width)


def plain_attention(queries, key_cache, value_cache, new_keys, new_values, cache_lengths):
    rows = queries.shape[0]
    length = key_cache.shape[1]
    scale = 1.0 / HD**0.5
    query = queries.reshape(rows, KVH, GROUP, HD)
    keys = key_cache.reshape(rows, length, KVH, HD)
    vals = value_cache.reshape(rows, length, KVH, HD)
    score = jnp.einsum("rkgh,rlkh->rkgl", query, keys, preferred_element_type=jnp.float32) * scale
    live = jnp.arange(length, dtype=jnp.int32)[None, :] < cache_lengths[:, None]
    score = jnp.where(live[:, None, None, :], score, -jnp.inf)
    own = (
        jnp.einsum(
            "rkgh,rkh->rkg",
            query,
            new_keys.reshape(rows, KVH, HD),
            preferred_element_type=jnp.float32,
        )
        * scale
    )
    top = jnp.maximum(jnp.max(score, axis=-1), own)
    weights = jnp.exp(score - top[..., None])
    own_weight = jnp.exp(own - top)
    total = jnp.sum(weights, axis=-1) + own_weight
    probs = (weights / total[..., None]).astype(jnp.bfloat16)
    own_prob = (own_weight / total).astype(jnp.bfloat16)
    mixed = jnp.einsum("rkgl,rlkh->rkgh", probs, vals, preferred_element_type=jnp.float32)
    mixed = mixed + own_prob.astype(jnp.float32)[..., None] * new_values.reshape(
        rows, KVH, 1, HD
    ).astype(jnp.float32)
    return mixed.reshape(rows, HEADS * HD).astype(jnp.bfloat16)


def plain_shards(
    moe_input,
    norm_gain,
    router_weight,
    routes,
    gate_weight,
    up_weight,
    down_weight,
    queries,
    key_cache,
    value_cache,
    new_keys,
    new_values,
    cache_lengths,
):
    rows, width = moe_input.shape
    experts = router_weight.shape[1]
    devices = lax.axis_size("node")
    slices = devices // experts
    capacity = rows // 2
    normed = normalize(moe_input, norm_gain)
    logits = jnp.dot(normed, router_weight, preferred_element_type=jnp.float32)
    onehot_int = (routes[:, :, None] == jnp.arange(experts, dtype=jnp.int32)[None, None, :]).astype(
        jnp.int32
    )
    onehot = onehot_int.astype(jnp.float32)
    picked = jnp.sum(onehot * logits[:, None, :], axis=-1)
    weight = 1.0 / (1.0 + jnp.exp(picked[:, ::-1] - picked))
    member_int = jnp.sum(onehot_int, axis=1)
    ranks_int = jnp.cumsum(member_int, axis=0) - member_int
    slots = jnp.arange(capacity, dtype=jnp.int32)
    select = (
        jnp.transpose(member_int)[:, None, :]
        * (jnp.transpose(ranks_int)[:, None, :] == slots[None, :, None]).astype(jnp.int32)
    ).astype(jnp.bfloat16)
    gate_slice = gate_weight[0]
    up_slice = up_weight[0]
    down_slice = down_weight[0]
    packed = jnp.einsum("ecr,rd->ecd", select, normed, preferred_element_type=jnp.float32).astype(
        jnp.bfloat16
    )
    outgoing = jnp.broadcast_to(packed[:, None], (experts, slices, capacity, width)).reshape(
        devices, capacity, width
    )
    summed = send_back(
        run_expert(
            lax.all_to_all(outgoing, "node", split_axis=0, concat_axis=0, tiled=True),
            gate_slice,
            up_slice,
            down_slice,
        ),
        experts,
        slices,
    )
    slot_of = jnp.sum(onehot_int * ranks_int[:, None, :], axis=-1)
    position = routes * capacity + slot_of
    picked_rows = summed.reshape(experts * capacity, width)[position]
    moe_output = jnp.sum(weight[:, :, None] * picked_rows, axis=1).astype(jnp.bfloat16)
    attention_output = plain_attention(
        queries, key_cache, value_cache, new_keys, new_values, cache_lengths
    )
    return (moe_output, attention_output)


def select_slots(routes, experts, capacity):
    lines, rows = experts.shape
    named = [routes[k : k + 1, :] == experts for k in range(2)]
    member = jnp.where(named[0] | named[1], 1.0, 0.0)
    before = lax.broadcasted_iota(jnp.int32, (rows, rows), 0) < lax.broadcasted_iota(
        jnp.int32, (rows, rows), 1
    )
    rank = jnp.dot(member, jnp.where(before, 1.0, 0.0), preferred_element_type=F32)
    slot = (lax.broadcasted_iota(jnp.int32, (lines, rows), 0) % capacity).astype(F32)
    return [flag & (rank == slot) for flag in named]


def line_experts(column, capacity, lines, rows):
    line = lax.broadcasted_iota(jnp.int32, (lines, rows), 0)
    block = 2 * capacity
    return ((line // block) ^ column) * 2 + (line % block) // capacity


def pack_kernel(capacity, x_hbm, routes_hbm, *refs):
    *out_refs, x_ref, routes_ref, sems = refs
    copies = [
        pltpu.make_async_copy(routes_hbm, routes_ref, sems.at[0]),
        pltpu.make_async_copy(x_hbm, x_ref, sems.at[1]),
    ]
    for copy in copies:
        copy.start()
    for copy in copies:
        copy.wait()
    column = lax.axis_index("node") // 4
    rows = x_ref.shape[0]
    block = out_refs[0].shape[0]
    lines = block * len(out_refs)
    first, second = select_slots(
        routes_ref[...], line_experts(column, capacity, lines, rows), capacity
    )
    chosen = jnp.where(first | second, 1.0, 0.0).astype(BF16)
    packed = jnp.dot(chosen, x_ref[...], preferred_element_type=F32)
    for k, out_ref in enumerate(out_refs):
        out_ref[...] = packed[k * block : (k + 1) * block].astype(BF16)


def far_first(columns):
    return sorted(range(columns), key=lambda k: (k < columns // 2, -k))


def back_order(columns):
    order = far_first(columns)
    return [order[0], order[2], order[1], *order[3:]]


def halves_kernel(capacity, *refs):
    *in_refs, _, keep_ref, send_ref = refs
    mine = (lax.axis_index("node") // 2) % 2
    block = 2 * capacity
    lines = len(in_refs) * block
    half = lines // 2
    out_line = lax.broadcasted_iota(jnp.int32, (lines, lines), 0)
    in_line = lax.broadcasted_iota(jnp.int32, (lines, lines), 1)
    which = jnp.where(out_line < half, mine, 1 - mine)
    within = out_line % half
    source = (within // capacity) * block + which * capacity + within % capacity
    move = jnp.where(in_line == source, 1.0, 0.0).astype(BF16)
    order = far_first(len(in_refs))
    values = jnp.concatenate([in_refs[order.index(k)][...] for k in range(len(order))], axis=0)
    moved = jnp.dot(move, values, preferred_element_type=F32)
    keep_ref[...] = moved[:half].astype(BF16)
    send_ref[...] = moved[half:].astype(BF16)


def merge_kernel(capacity, own_ref, far_ref, *out_refs):
    block = 2 * capacity
    lines = block * len(out_refs)
    out_line = lax.broadcasted_iota(jnp.int32, (lines, lines), 0)
    in_line = lax.broadcasted_iota(jnp.int32, (lines, lines), 1)
    which = (out_line % block) // capacity
    source = which * (lines // 2) + (out_line // block) * capacity + out_line % capacity
    move = jnp.where(in_line == source, 1.0, 0.0).astype(BF16)
    values = (own_ref[...] + far_ref[...].astype(F32)).astype(BF16)
    moved = jnp.dot(move, values, preferred_element_type=F32)
    for k, out_ref in enumerate(out_refs):
        out_ref[...] = moved[k * block : (k + 1) * block].astype(BF16)


def rms(values, gain):
    wide = values.astype(F32)
    meansq = jnp.mean(wide * wide, axis=-1, keepdims=True)
    return (wide * lax.rsqrt(meansq + 1e-05) * gain.astype(F32).reshape(1, -1)).astype(BF16)


def attention(lengths_ref, q_ref, k_ref, v_ref, nk_ref, nv_ref, out_ref):
    rows = q_ref.shape[0]
    length = k_ref.shape[1]
    groups = k_ref.shape[2] // HD
    per_group = q_ref.shape[1] // HD // groups
    lines, columns = per_group * rows, rows * length
    scale = 1.0 / HD**0.5
    row = lax.broadcasted_iota(jnp.int32, (lines, 1), 0) % rows
    count = jnp.zeros((lines, 1), jnp.int32)
    for r in range(rows):
        count = jnp.where(row == r, lengths_ref[r], count)
    position = lax.broadcasted_iota(jnp.int32, (lines, columns), 1) - row * length
    live = (position >= 0) & (position < count)
    for g in range(groups):
        lanes = slice(g * HD, (g + 1) * HD)
        heads = [slice(h * HD, (h + 1) * HD) for h in range(g * per_group, (g + 1) * per_group)]
        query = jnp.concatenate([q_ref[:, head].astype(F32) for head in heads], axis=0)
        keys = k_ref[:, :, lanes].reshape(columns, HD)
        values = v_ref[:, :, lanes].reshape(columns, HD)
        new_key = jnp.concatenate([nk_ref[:, lanes].astype(F32)] * per_group, axis=0)
        new_value = jnp.concatenate([nv_ref[:, lanes].astype(F32)] * per_group, axis=0)
        score = (
            lax.dot_general(
                query.astype(BF16), keys, (((1,), (1,)), ((), ())), preferred_element_type=F32
            )
            * scale
        )
        own = jnp.sum(query * new_key, axis=-1, keepdims=True) * scale
        score = jnp.where(live, score, -jnp.inf)
        top = jnp.maximum(jnp.max(score, axis=-1, keepdims=True), own)
        weights = jnp.exp(score - top)
        own_weight = jnp.exp(own - top)
        total = jnp.sum(weights, axis=-1, keepdims=True) + own_weight
        probs = (weights / total).astype(BF16)
        own_prob = (own_weight / total).astype(BF16).astype(F32)
        mixed = jnp.dot(probs, values, preferred_element_type=F32) + own_prob * new_value
        for j, head in enumerate(heads):
            out_ref[:, head] = mixed[j * rows : (j + 1) * rows].astype(BF16)


def attend_kernel(lengths_ref, q_ref, k_ref, v_ref, nk_ref, nv_ref, _, out_ref):
    attention(lengths_ref, q_ref, k_ref, v_ref, nk_ref, nv_ref, out_ref)


def weigh_kernel(capacity, x_ref, gain_ref, router_ref, routes_ref, table_ref):
    logits = lax.dot_general(
        router_ref[...],
        rms(x_ref[...], gain_ref[...]),
        (((1,), (1,)), ((), ())),
        preferred_element_type=F32,
    )
    table_ref[...] = slot_weights(capacity, routes_ref[...], logits, table_ref.shape[0])


def down_copy(down_ref, buf, sems, tile, slot):
    return pltpu.make_async_copy(
        down_ref.at[0, pl.ds(pl.multiple_of(tile * TILE, TILE), TILE), :],
        buf.at[slot],
        sems.at[slot],
    )


def expert_kernel(
    slots,
    a_ref,
    b_ref,
    c_ref,
    d_ref,
    gain_ref,
    gate_ref,
    up_ref,
    down_ref,
    own_ref,
    far_ref,
    x_buf,
    total,
    down_buf,
    sems,
):
    tiles = gate_ref.shape[2] // TILE
    part = a_ref.shape[0]
    lines = total.shape[0]
    for tile in range(min(slots, tiles)):
        down_copy(down_ref, down_buf, sems, tile, tile).start()
    for i, ref in enumerate((a_ref, b_ref, c_ref, d_ref)):
        x_buf[i * part : (i + 1) * part, :] = rms(ref[...], gain_ref[...])
    x_buf[lines:, :] = jnp.zeros_like(x_buf[lines:, :])

    def activate(tile):
        cols = slice(tile * TILE, (tile + 1) * TILE)
        x = x_buf[...]
        gated = jnp.dot(x, gate_ref[0, :, cols], preferred_element_type=F32)
        upper = jnp.dot(x, up_ref[0, :, cols], preferred_element_type=F32)
        return (gated / (1.0 + jnp.exp(-gated)) * upper).astype(BF16)

    ready = activate(0)
    for tile in range(tiles):
        down_copy(down_ref, down_buf, sems, tile, tile % slots).wait()
        product = jnp.dot(ready, down_buf[tile % slots], preferred_element_type=F32)[:lines]
        if tile + 1 < tiles:
            ready = activate(tile + 1)
            total[...] = product if tile == 0 else total[...] + product
        if tile + slots < tiles:
            down_copy(down_ref, down_buf, sems, tile + slots, tile % slots).start()
    result = total[...] + product if tiles > 1 else product
    own_ref[...] = result[: 2 * part]
    far_ref[...] = result[2 * part :].astype(BF16)


def slot_weights(capacity, routes, logits, lines):
    column, mine = lax.axis_index("node") // 4, (lax.axis_index("node") // 2) % 2
    shape = (lines, routes.shape[1])
    line = lax.broadcasted_iota(jnp.int32, shape, 0)
    block = 2 * capacity
    which = (line % block) // capacity
    experts = ((line // block) ^ column) * 2 + jnp.where(which == 0, mine, 1 - mine)
    expert = lax.broadcasted_iota(jnp.int32, logits.shape, 0)
    picked = [
        jnp.sum(jnp.where(routes[k : k + 1, :] == expert, logits, 0.0), axis=0, keepdims=True)
        for k in range(2)
    ]
    hits = select_slots(routes, experts, capacity)
    table = jnp.zeros(shape, F32)
    for k in range(2):
        weight = 1.0 / (1.0 + jnp.exp(picked[1 - k] - picked[k]))
        table += jnp.where(hits[k], weight, 0.0)
    return table


def mix_kernel(capacity, table_ref, other_ref, *refs):
    *in_refs, own_ref, send_ref = refs
    which = lax.broadcasted_iota(jnp.int32, table_ref.shape, 0) % (2 * capacity) // capacity
    table = jnp.concatenate(
        [
            jnp.where(which == 0, table_ref[...], 0.0),
            jnp.where(which == 1, other_ref[...], 0.0),
        ],
        axis=1,
    )
    high = table.astype(BF16)
    rest = table - high.astype(F32)
    middle = rest.astype(BF16)
    low = (rest - middle.astype(F32)).astype(BF16)
    order = back_order(len(in_refs))
    values = jnp.concatenate([in_refs[order.index(k)][...] for k in range(len(order))], axis=0)
    terms = [
        lax.dot_general(term, values, (((0,), (0,)), ((), ())), preferred_element_type=F32)
        for term in (low, middle, high)
    ]
    mixed = terms[0] + terms[1] + terms[2]
    rows = own_ref.shape[0]
    own_ref[...] = mixed[:rows]
    send_ref[...] = mixed[rows:].astype(BF16)


def final_kernel(own_ref, other_ref, _, out_ref):
    out_ref[...] = (own_ref[...] + other_ref[...].astype(F32)).astype(BF16)


def call(kernel, name, outs, ins, operands, scratch=(), limit=4, cost=None):
    return pl.pallas_call(
        kernel,
        out_shape=outs,
        in_specs=ins,
        out_specs=tuple(WHOLE for _ in outs) if isinstance(outs, tuple) else WHOLE,
        scratch_shapes=list(scratch),
        compiler_params=pltpu.CompilerParams(vmem_limit_bytes=limit * MIB),
        cost_estimate=cost,
        name=name,
    )(*operands)


def exchange(values, bits):
    size = lax.axis_size("node")
    return lax.ppermute(values, "node", [(i, i ^ bits) for i in range(size)])


def paired_shards(
    moe_input,
    norm_gain,
    router_weight,
    routes,
    gate_weight,
    up_weight,
    down_weight,
    queries,
    key_cache,
    value_cache,
    new_keys,
    new_values,
    cache_lengths,
):
    rows, width = moe_input.shape
    capacity = rows // 2
    columns = lax.axis_size("node") // 4
    block = 2 * capacity
    half = columns * capacity
    named = routes.T
    gain = norm_gain

    def like(lines, dtype=BF16):
        return jax.ShapeDtypeStruct((lines, width), dtype)

    def held(lines, dtype=BF16):
        return pltpu.VMEM((lines, width), dtype)

    packed = call(
        functools.partial(pack_kernel, capacity),
        "pack",
        (like(block),) * columns,
        [pl.BlockSpec(memory_space=pltpu.HBM)] * 2,
        [pltpu.with_memory_space_constraint(array, pltpu.HBM) for array in (moe_input, named)],
        [
            pltpu.VMEM(moe_input.shape, BF16),
            pltpu.VMEM(named.shape, jnp.int32),
            pltpu.SemaphoreType.DMA((2,)),
        ],
        cost=pl.CostEstimate(flops=10**11, bytes_accessed=64 * MIB, transcendentals=0),
    )
    blocks = [exchange(packed[k], 4 * k) if k else packed[k] for k in far_first(columns)]
    (table,) = call(
        functools.partial(weigh_kernel, capacity),
        "weigh",
        (jax.ShapeDtypeStruct((columns * block, rows), F32),),
        [WHOLE] * 4,
        (moe_input, gain, router_weight.T, named),
    )
    keep, send = call(
        functools.partial(halves_kernel, capacity),
        "halves",
        (like(half),) * 2,
        [WHOLE] * columns + [ANY],
        (*blocks, table),
    )
    far_keep = exchange(keep, 1)
    across = exchange(send, 2)
    other_table = exchange(table, 2)
    far_across = exchange(across, 1)
    slots = 2
    lines = max(4 * half, 128)
    own, far = call(
        functools.partial(expert_kernel, slots),
        "expert",
        (held(2 * half, F32), held(2 * half)),
        [WHOLE] * 7 + [ANY],
        (
            *[
                pltpu.with_memory_space_constraint(part, pltpu.VMEM)
                for part in (keep, across, far_keep, far_across)
            ],
            gain,
            pltpu.with_memory_space_constraint(gate_weight, pltpu.VMEM),
            pltpu.with_memory_space_constraint(up_weight, pltpu.VMEM),
            down_weight,
        ),
        [
            pltpu.VMEM((lines, width), BF16),
            pltpu.VMEM((4 * half, width), F32),
            pltpu.VMEM((slots, TILE, width), BF16),
            pltpu.SemaphoreType.DMA((slots,)),
        ],
        limit=12,
    )
    sums = call(
        functools.partial(merge_kernel, capacity),
        "merge",
        (like(block),) * columns,
        [WHOLE] * 2,
        (pltpu.with_memory_space_constraint(own, pltpu.VMEM), exchange(far, 1)),
    )
    results = [exchange(sums[k], 4 * k) if k else sums[k] for k in back_order(columns)]
    mine, theirs = call(
        functools.partial(mix_kernel, capacity),
        "mix",
        (held(rows, F32), like(rows)),
        [WHOLE] * (2 + columns),
        (table, other_table, *results),
    )
    (attended,) = call(
        attend_kernel,
        "attend",
        (pltpu.HBM((rows, width), BF16),),
        [pl.BlockSpec(memory_space=pltpu.SMEM)] + [WHOLE] * 5 + [ANY],
        (cache_lengths, queries, key_cache, value_cache, new_keys, new_values, theirs),
        cost=pl.CostEstimate(flops=10**8, bytes_accessed=4 * MIB, transcendentals=0),
    )
    moe_output = call(
        final_kernel,
        "final",
        like(rows),
        [WHOLE] * 2 + [pl.BlockSpec(memory_space=pltpu.HBM)],
        (
            pltpu.with_memory_space_constraint(mine, pltpu.VMEM),
            exchange(theirs, 2),
            pltpu.with_memory_space_constraint(attended, pltpu.HBM),
        ),
    )
    return moe_output, attended


def shards(*arrays):
    experts = arrays[2].shape[1]
    devices = lax.axis_size("node")
    units = arrays[4].shape[2]
    if devices == 2 * experts and devices % 16 == 0 and units % TILE == 0 and arrays[0].shape[0] == 8:
        return paired_shards(*arrays)
    return plain_shards(*arrays)


def solution(mesh):
    in_specs = (
        P(("groups", "node"), None),
        P(),
        P(),
        P(("groups", "node"), None),
        P("node", None, None),
        P("node", None, None),
        P("node", None, None),
        P(("groups", "node"), None),
        P(("groups", "node"), None, None),
        P(("groups", "node"), None, None),
        P(("groups", "node"), None),
        P(("groups", "node"), None),
        P(("groups", "node")),
    )
    out_specs = (P(("groups", "node"), None), P(("groups", "node"), None))
    return jax.shard_map(shards, mesh=mesh, in_specs=in_specs, out_specs=out_specs, check_vma=False)
```
